32 devices in a mesh: groups: 2 (over x), cluster: 16 (over z, y, core).
Axes of the slice: x: 2, y: 2, z: 4, core: 2. Of those that a mesh axis runs over, the one named last changes fastest.
Arguments:
- embed: bfloat16 [32768, 768], P(('groups', 'cluster')), parts along dimension 0, may hold values from -6 to 6
- valid: int32 [32768], P(('groups', 'cluster')), parts along dimension 0, may hold values from 0 to 1, as said below
- pairs: int32 [224, 2], P(('groups', 'cluster')), parts along dimension 0, may hold values from 0 to 31, as said below
- pair_count: int32 [32], P(('groups', 'cluster')), parts along dimension 0, may hold values from 1 to 7, as said below
Outputs:
- log_density: float32 [32768], P(('groups', 'cluster')), parts along dimension 0
- neighbour_sum: bfloat16 [32768, 768], P(('groups', 'cluster')), parts along dimension 0
The draws below stay inside these ranges and needn't reach their ends.
There are 2 independent parts, one for each index of `groups`. The reference program is written for one: setup_inputs(seed, part) draws one part's arguments, and reference() takes and returns one part's arrays. A program takes and returns all parts, laid end to end along the dimension named above; each array names one. Nothing has to cross between parts.
Inputs may be any that keep to these rules, and one draw needn't show every extreme that they name: `pairs`: clusters are runs of 1 to 4 consecutive blocks. The live slots of index d list, each once, every pair (i, j) with i <= j of blocks of one cluster whose first block i is held by d (i // 2 == d); so j // 2 - d is 0 to 2, and this bound is reached. Dead slots hold arbitrary blocks of d. `pair_count`: some index has all 7 slots live. `valid`: in each block the real rows come first and there is at least one; only the last block of a cluster has padding.
All inputs are finite; a program needn't handle non-finite values.
Results may differ from the reference program's by a relative error of at most 0.007.
Values may be sent and summed in bfloat16 or wider, within the bound.
No kernel may reach another device: no remote copies, remote signals or barrier semaphores. Data moves between devices by JAX's collectives and lax.ppermute only.
A program may use at most 64 MiB of HBM per device.

```python
import jax
import jax.numpy as jnp
from jax import lax

D = 768
BLOCK = 512
BLK_DEV = 2
SPAN = 4
PAIRS_DEV = 7
BLOCKS = 32
ROWS = 16384


def cluster_member(key):
    sizes = jax.random.randint(key, (BLOCKS,), 1, SPAN + 1)
    sizes = sizes.at[0].set(SPAN).at[1].set(1).at[2].set(SPAN)
    ends = jnp.cumsum(sizes)
    index = jnp.arange(BLOCKS, dtype=jnp.int32)
    return jnp.sum((ends[None, :] <= index[:, None]).astype(jnp.int32), axis=1)


def pair_table(member):
    owners = BLOCKS // BLK_DEV
    devices = jnp.arange(owners, dtype=jnp.int32)
    inner = jnp.arange(BLK_DEV, dtype=jnp.int32)
    steps = jnp.arange(SPAN, dtype=jnp.int32)
    first = devices[:, None, None] * BLK_DEV + inner[None, :, None] + 0 * steps[None, None, :]
    second = first + steps[None, None, :]
    safe = jnp.minimum(second, BLOCKS - 1)
    live = jnp.logical_and(second < BLOCKS, member[safe] == member[first])
    first = first.reshape(owners, BLK_DEV * SPAN)
    second = second.reshape(owners, BLK_DEV * SPAN)
    live = live.reshape(owners, BLK_DEV * SPAN).astype(jnp.int32)
    order = jnp.argsort(1 - live, axis=1, stable=True)
    first = jnp.take_along_axis(first, order, axis=1)[:, :PAIRS_DEV]
    second = jnp.take_along_axis(second, order, axis=1)[:, :PAIRS_DEV]
    live = jnp.take_along_axis(live, order, axis=1)[:, :PAIRS_DEV]
    filler = devices[:, None] * BLK_DEV + 0 * first
    first = jnp.where(live > 0, first, filler)
    second = jnp.where(live > 0, second, filler)
    table = jnp.stack([first, second], axis=-1).reshape(owners * PAIRS_DEV, 2)
    return (table.astype(jnp.int32), jnp.sum(live, axis=1).astype(jnp.int32))


def mixed_rows(keys, group, noise, share):
    centers = jax.random.normal(keys[0], (BLOCKS, D), jnp.float32)
    branches = jax.random.normal(keys[1], (BLOCKS * 4, D), jnp.float32)
    pick = jax.random.randint(keys[2], (ROWS,), 0, 4)
    side = jax.random.uniform(keys[5], (ROWS, 1), jnp.float32, 0.0, 0.4)
    rest = jnp.sqrt(jnp.maximum(1.0 - share * share - side * side, 0.02))
    rows = share * centers[group] + side * branches[group * 4 + pick] + rest * noise
    copied = jax.random.randint(keys[6], (ROWS, 1), 0, 4) == 0
    extra = jax.random.normal(keys[7], (ROWS, D), jnp.float32)
    before = jnp.roll(rows, 1, axis=0)
    rows = jnp.where(copied, 0.98 * before + 0.2 * extra, rows)
    return jnp.clip(rows, -6.0, 6.0)


def draw_embed(key, part):
    member = cluster_member(key)
    key = jax.random.fold_in(key, 11)
    keys = jax.random.split(key, 8)
    row_block = jnp.arange(ROWS, dtype=jnp.int32) // BLOCK
    group = member[row_block]
    noise = jax.random.normal(keys[3], (ROWS, D), jnp.float32)
    share = jax.random.uniform(keys[4], (ROWS, 1), jnp.float32, 0.3, 0.9)
    return mixed_rows(keys, group, noise, share).astype(jnp.bfloat16)


def draw_pairs(key, part):
    member = cluster_member(key)
    table, counts = pair_table(member)
    return table


def draw_pair_count(key, part):
    member = cluster_member(key)
    table, counts = pair_table(member)
    return counts


def draw_valid(key, part):
    member = cluster_member(key)
    key = jax.random.fold_in(key, 7)
    closing = jnp.concatenate([member[1:] != member[:-1], jnp.ones((1,), dtype=bool)])
    filled = jax.random.randint(key, (BLOCKS,), 1, BLOCK + 1)
    counts = jnp.where(closing, filled, BLOCK)
    rows = jnp.arange(BLOCK, dtype=jnp.int32)
    return (rows[None, :] < counts[:, None]).astype(jnp.int32).reshape(BLOCKS * BLOCK)


def setup_inputs(seed: int = 0, part: int = 0) -> dict:
    key_list = jax.random.split(jax.random.key(seed), 5)
    part_keys = jax.random.split(jax.random.fold_in(key_list[4], part), 5)
    return {
        "embed": draw_embed(jax.random.fold_in(jax.random.fold_in(key_list[4], part), 71), part),
        "valid": draw_valid(jax.random.fold_in(jax.random.fold_in(key_list[4], part), 71), part),
        "pairs": draw_pairs(jax.random.fold_in(jax.random.fold_in(key_list[4], part), 71), part),
        "pair_count": draw_pair_count(jax.random.fold_in(jax.random.fold_in(key_list[4], part), 71), part),
    }


sharpness = 8.0

def normalize(embed):
    wide = embed.astype(jnp.float32)
    scale = lax.rsqrt(lax.optimization_barrier(jnp.mean(wide * wide, axis=-1, keepdims=True)) + 1e-06)
    return (wide * scale).astype(jnp.bfloat16)

def kernel(left, right):
    gram = lax.dot_general(left, right, (((1,), (1,)), ((), ())), preferred_element_type=jnp.float32)
    return jnp.exp(sharpness * (gram / left.shape[1] - 1.0))

def reference(embed, valid, pairs, pair_count):
    normed = normalize(embed).reshape(BLOCKS, BLOCK, D)
    weight = valid.astype(jnp.float32).reshape(BLOCKS, BLOCK)
    mask_b = valid.astype(jnp.bfloat16).reshape(BLOCKS, BLOCK)
    slots = jnp.arange(pairs.shape[0], dtype=jnp.int32)
    live = slots % PAIRS_DEV < pair_count[slots // PAIRS_DEV]

    def visit(carry, item):
        first, second, active = item

        def work(state):
            density, sums = state
            left = normed[first]
            right = normed[second]
            kern = kernel(left, right)
            rounded = kern.astype(jnp.bfloat16)
            row_dens = lax.optimization_barrier(jnp.sum(kern * weight[second][None, :], axis=1))
            row_sums = jnp.dot(rounded * mask_b[second][None, :], right, preferred_element_type=jnp.float32)
            col_dens = lax.optimization_barrier(jnp.sum(kern * weight[first][:, None], axis=0))
            col_sums = lax.dot_general(rounded * mask_b[first][:, None], left, (((0,), (0,)), ((), ())), preferred_element_type=jnp.float32)
            cross = (first != second).astype(jnp.float32)
            density = density.at[first].add(row_dens)
            density = density.at[second].add(cross * col_dens)
            sums = sums.at[first].add(row_sums)
            sums = sums.at[second].add(cross * col_sums)
            return (density, sums)
        return (lax.cond(active, work, lambda state: state, carry), None)
    start = (jnp.zeros((BLOCKS, BLOCK), jnp.float32), jnp.zeros((BLOCKS, BLOCK, D), jnp.float32))
    (density, sums), _ = lax.scan(visit, start, (pairs[:, 0].astype(jnp.int32), pairs[:, 1].astype(jnp.int32), live))
    safe = jnp.where(weight > 0.5, density, 1.0)
    log_density = jnp.where(weight > 0.5, jnp.log(safe), 0.0).reshape(ROWS)
    neighbour_sum = (sums * weight[:, :, None]).astype(jnp.bfloat16).reshape(ROWS, D)
    return (log_density, neighbour_sum)
```

```python
import functools

import jax
import jax.numpy as jnp
from jax import lax
from jax.experimental import pallas as pl
from jax.experimental.pallas import tpu as pltpu
from jax.sharding import PartitionSpec as P

BLOCK = 512
HALF = BLOCK // 2
TILE = 16
LANES = 128
MARK = 100.0
SHARPNESS = 8.0
LOG2E = 1.4426950408889634

IDX, PAR, V0, V1, E0, E1, C0, C1 = range(8)

VM = pl.BlockSpec(memory_space=pltpu.VMEM)
SM = pl.BlockSpec(memory_space=pltpu.SMEM)


def iota(shape, dim):
    return lax.broadcasted_iota(jnp.int32, shape, dim)


def normalized(rows):
    wide = rows.astype(jnp.float32)
    scale = lax.rsqrt(jnp.mean(wide * wide, axis=-1, keepdims=True) + 1e-06)
    return wide * scale


def marked(rows, count):
    mark = jnp.where(iota(rows.shape, 1) == 0, MARK, 0.0)
    return jnp.where(iota(rows.shape, 0) < count, rows, mark).astype(jnp.bfloat16)


def real_rows(ref, start, rows):
    head = ref[pl.ds(start, rows), 0:LANES].astype(jnp.float32)
    real = jnp.logical_and(iota(head.shape, 1) == 0, head < 0.5 * MARK)
    return jnp.sum(jnp.where(real, 1.0, 0.0)).astype(jnp.int32)


def at(block):
    return pl.multiple_of(block * BLOCK, BLOCK)


def kernel_tile(left, right, count):
    gram = lax.dot_general(
        left, right, (((1,), (1,)), ((), ())), preferred_element_type=jnp.float32
    )
    scale = SHARPNESS * LOG2E / left.shape[1]
    kern = jnp.exp2(gram * scale - SHARPNESS * LOG2E)
    return jnp.where(iota(kern.shape, 1) < count, kern, 0.0)


def folded(kern):
    return functools.reduce(
        jnp.add, [kern[:, c : c + LANES] for c in range(0, kern.shape[1], LANES)]
    )


def terms(left, right, count):
    kern = kernel_tile(left, right, count)
    sums = jnp.dot(kern.astype(jnp.bfloat16), right, preferred_element_type=jnp.float32)
    return folded(kern), sums


def add_terms(x_ref, row, right, count, dens_ref, acc_ref):
    dens, sums = terms(x_ref[pl.ds(row, BLOCK), :], right, count)
    dens_ref[pl.ds(row, BLOCK), :] += dens
    acc_ref[pl.ds(row, BLOCK), :] += sums


def sibling_links(s, sib_ref):
    tile = sib_ref[pl.ds(2 * BLOCK, TILE), 0:LANES].astype(jnp.float32)
    lane = iota(tile.shape, 1)
    inner = jnp.max(jnp.where(lane == 0, tile, 0.0)) > 0.5
    outer = jnp.max(jnp.where(lane == 1, tile, 0.0)) > 0.5
    return inner, outer


def joined(s, outer):
    return jnp.where(s[PAR] == 1, outer.astype(jnp.int32), s[E1]) == 1


def prepare_kernel(idx_ref, pairs_ref, count_ref, embed_ref, valid_ref, s_ref, first_ref):
    idx = idx_ref[0]
    par = idx % 2
    base = idx * 2
    counts = [jnp.int32(0), jnp.int32(0)]
    for slot in range(pairs_ref.shape[0]):
        live = slot < count_ref[0]
        for b in range(2):
            hit = jnp.logical_and(live, pairs_ref[slot, 0] == base + b)
            counts[b] = counts[b] + hit.astype(jnp.int32)
    per = valid_ref.shape[0] // 2
    reals = [
        jnp.sum(valid_ref[b * per : (b + 1) * per, :].astype(jnp.float32)).astype(jnp.int32)
        for b in range(2)
    ]
    links = [(c >= 2).astype(jnp.int32) for c in counts]
    s_ref[IDX] = idx
    s_ref[PAR] = par
    for b in range(2):
        s_ref[V0 + b] = reals[b]
        s_ref[E0 + b] = links[b]
        s_ref[C0 + b] = counts[b]
    near = jnp.where(par == 1, reals[1] * links[1], reals[0])
    rows = embed_ref[pl.ds(at(par), HALF), :]
    first_ref[...] = marked(normalized(rows), near)


def normalize_kernel(s, embed_ref, x_ref, second_ref):
    for part in range(4):
        rows = slice(part * HALF, (part + 1) * HALF)
        count = s[V0 + part // 2] - (part % 2) * HALF
        x_ref[rows, :] = marked(normalized(embed_ref[rows, :]), count)
    lane = iota((TILE, x_ref.shape[1]), 1)
    flags = jnp.where(
        lane == 0,
        s[E0].astype(jnp.float32),
        jnp.where(lane == 1, s[E1].astype(jnp.float32), 0.0),
    )
    x_ref[2 * BLOCK :, :] = flags.astype(jnp.bfloat16)
    near = at(s[PAR]) + HALF
    keep = jnp.logical_or(s[PAR] == 0, s[E1] == 1)
    rows = x_ref[pl.ds(near, HALF), :].astype(jnp.float32)
    second_ref[...] = marked(rows, jnp.where(keep, BLOCK, 0))


def own_kernel(s, x_ref, dens_ref, acc_ref):
    for b in range(2):
        rows = x_ref[b * BLOCK : (b + 1) * BLOCK, :]
        dens, sums = terms(rows, rows, s[V0 + b])
        dens_ref[b * BLOCK : (b + 1) * BLOCK, :] = dens
        acc_ref[b * BLOCK : (b + 1) * BLOCK, :] = sums

    @pl.when(s[E0] == 1)
    def _():
        for b in range(2):
            other = x_ref[(1 - b) * BLOCK : (2 - b) * BLOCK, :]
            add_terms(x_ref, b * BLOCK, other, s[V0 + 1 - b], dens_ref, acc_ref)


def sibling_kernel(s, x_ref, sib_ref, dens_in, acc_in, dens_ref, acc_ref):
    inner, outer = sibling_links(s, sib_ref)
    near, far = at(s[PAR]), at(1 - s[PAR])

    @pl.when(joined(s, outer))
    def _():
        def column(start):
            count = real_rows(sib_ref, start, BLOCK)
            right = sib_ref[pl.ds(start, BLOCK), :]
            add_terms(x_ref, far, right, count, dens_ref, acc_ref)

            @pl.when(s[E0] == 1)
            def _():
                add_terms(x_ref, near, right, count, dens_ref, acc_ref)

        column(near)
        pl.when(inner)(lambda: column(far))


def partial_sums(s, half, q_ref, x_ref, sib_ref, out_ref, dens_ref):
    inner, outer = sibling_links(s, sib_ref)
    near, far = at(s[PAR]), at(1 - s[PAR])
    sums_go = jnp.where(s[PAR] == 1, s[C1] == 2, s[C0] == 3)

    @pl.when(sums_go)
    def _():
        left = q_ref[...]
        count = jnp.where(s[PAR] == 1, s[V0], s[V1]) * s[E0]
        dens, sums = terms(left, x_ref[pl.ds(far, BLOCK), :], count)
        use = jnp.logical_and(s[E0] == 1, joined(s, outer))
        count = jnp.where(use, real_rows(sib_ref, near, BLOCK), 0)
        more_dens, more_sums = terms(left, sib_ref[pl.ds(near, BLOCK), :], count)
        dens_ref[...] = dens + more_dens
        out_ref[0:HALF, :] = (sums + more_sums).astype(jnp.bfloat16)

    @pl.when(jnp.logical_not(sums_go))
    def _():
        dens_ref[...] = jnp.zeros_like(dens_ref)
        keep = jnp.logical_and(s[E0] == 1, jnp.logical_or(s[PAR] == 0, s[E1] == 1))
        rows = x_ref[pl.ds(far + half * HALF, HALF), :].astype(jnp.float32)
        out_ref[0:HALF, :] = marked(rows, jnp.where(keep, BLOCK, 0))


def along_lanes(dens):
    return jnp.sum(dens.T, axis=0, keepdims=True)


def third_kernel(s, q_ref, x_ref, sib_ref, out_ref, dens_ref):
    partial_sums(s, 0, q_ref, x_ref, sib_ref, out_ref, dens_ref)


def fourth_kernel(s, q_ref, x_ref, sib_ref, dens_a_ref, out_ref, dens_ref):
    partial_sums(s, 1, q_ref, x_ref, sib_ref, out_ref, dens_ref)
    width = out_ref.shape[1]
    both = [along_lanes(dens_a_ref[...]), along_lanes(dens_ref[...])]
    row = jnp.concatenate(both + [jnp.zeros((1, width - BLOCK), jnp.float32)], axis=1)
    place = iota((TILE, width), 0)
    tile = jnp.zeros((TILE, width), jnp.float32)
    for piece in range(3):
        rounded = row.astype(jnp.bfloat16).astype(jnp.float32)
        tile = jnp.where(place == piece, rounded, tile)
        row = row - rounded
    out_ref[HALF:, :] = tile.astype(jnp.bfloat16)


def across(s, qa_ref):
    below = jnp.logical_and(s[IDX] > 0, real_rows(qa_ref, 0, HALF) > 0)
    return jnp.where(s[PAR] == 1, s[E1] == 1, below)


def near_kernel(s, n, x_ref, sib_ref, qa_ref, qb_ref, fa_ref, fb_ref, dens_in, acc_in, dens_ref, acc_ref):
    near, far = at(s[PAR]), at(1 - s[PAR])

    @pl.when(across(s, qa_ref))
    def _():
        for ref in (qa_ref, qb_ref):
            count = real_rows(ref, 0, HALF)
            add_terms(x_ref, near, ref[...], count, dens_ref, acc_ref)

            @pl.when(s[E0] == 1)
            def _():
                add_terms(x_ref, far, ref[...], count, dens_ref, acc_ref)

    inner, outer = sibling_links(s, sib_ref)
    beyond = jnp.where(s[PAR] == 1, (s[IDX] > 1).astype(jnp.int32), outer.astype(jnp.int32)) == 1
    reached = jnp.logical_and(jnp.logical_and(joined(s, outer), inner), beyond)
    reached = jnp.logical_and(reached, real_rows(fa_ref, 0, HALF) > 0)

    @pl.when(reached)
    def _():
        for ref in (fa_ref, fb_ref):
            count = real_rows(ref, 0, HALF)
            add_terms(x_ref, far, ref[...], count, dens_ref, acc_ref)


def take(s, half, x_ref, qa_ref, q_ref, dens_ref, acc_ref):
    near, far = at(s[PAR]), at(1 - s[PAR])
    linked = across(s, qa_ref)
    sums_came = jnp.where(s[PAR] == 1, s[C1] == 4, jnp.logical_and(linked, s[E0] == 0))
    rows_came = jnp.where(s[PAR] == 1, s[C1] == 3, jnp.logical_and(linked, s[E0] == 1))

    @pl.when(sums_came)
    def _():
        acc_ref[pl.ds(near + half * HALF, HALF), :] += q_ref[0:HALF, :].astype(jnp.float32)

    @pl.when(rows_came)
    def _():
        count = real_rows(q_ref, 0, HALF)

        @pl.when(count > 0)
        def _():
            add_terms(x_ref, near, q_ref[0:HALF, :], count, dens_ref, acc_ref)

            @pl.when(s[E0] == 1)
            def _():
                add_terms(x_ref, far, q_ref[0:HALF, :], count, dens_ref, acc_ref)

    return sums_came


def far_kernel(s, x_ref, qa_ref, q_ref, dens_in, acc_in, dens_ref, acc_ref):
    take(s, 0, x_ref, qa_ref, q_ref, dens_ref, acc_ref)


def last_kernel(s, x_ref, qa_ref, q_ref, dens_in, acc_in, log_ref, out_ref, dens_ref, acc_ref):
    sums_came = take(s, 1, x_ref, qa_ref, q_ref, dens_ref, acc_ref)
    tile = q_ref[HALF:, :].astype(jnp.float32)
    came = jnp.sum(jnp.where(iota(tile.shape, 0) < 3, tile, 0.0), axis=0, keepdims=True)
    for b in range(2):
        rows = slice(b * BLOCK, (b + 1) * BLOCK)
        count = s[V0 + b]
        density = along_lanes(dens_ref[rows, :])
        use = jnp.logical_and(sums_came, s[PAR] == b)
        density = density + jnp.where(use, came[:, 0:BLOCK], 0.0)
        real = iota(density.shape, 1) < count
        logs = jnp.where(real, jnp.log(jnp.where(real, density, 1.0)), 0.0)
        per = BLOCK // LANES
        for part in range(per):
            log_ref[b * per + part : b * per + part + 1, :] = logs[:, part * LANES : (part + 1) * LANES]
        sums = acc_ref[rows, :]
        out_ref[rows, :] = jnp.where(iota(sums.shape, 0) < count, sums, 0.0).astype(jnp.bfloat16)


def call(kernel, n_scalars, operands, outs, aliases=None, flops=0):
    specs = [SM] * n_scalars + [VM] * (len(operands) - n_scalars)
    out_specs = [SM if o.dtype == jnp.int32 else VM for o in outs]
    return pl.pallas_call(
        kernel,
        in_specs=specs,
        out_specs=out_specs,
        out_shape=outs,
        input_output_aliases=aliases or {},
        compiler_params=pltpu.CompilerParams(vmem_limit_bytes=16 << 20),
        cost_estimate=pl.CostEstimate(
            flops=int(flops), bytes_accessed=1 << 20, transcendentals=0
        ),
    )(*operands)


def per_device(embed, valid, pairs, pair_count):
    width = embed.shape[1]
    n = lax.axis_size("cluster")
    idx = lax.axis_index("cluster").astype(jnp.int32).reshape(1)
    chips = n // 2
    inchip = [(2 * c + k, 2 * c + 1 - k) for c in range(chips) for k in range(2)]
    edges = [(2 * c + 1, 2 * c + 2) for c in range(chips - 1)]
    edges = edges + [(b, a) for a, b in edges]

    def over_edge(block):
        return lax.ppermute(block, "cluster", edges)

    def to_sibling(block):
        return lax.ppermute(block, "cluster", inchip)

    bf16 = lambda rows: jax.ShapeDtypeStruct((rows, width), jnp.bfloat16)
    f32 = lambda rows, cols: jax.ShapeDtypeStruct((rows, cols), jnp.float32)
    state = [f32(2 * BLOCK, LANES), f32(2 * BLOCK, width)]
    pair = 4.0 * BLOCK * BLOCK * width
    valid = valid.reshape(-1, LANES)

    table, first = call(
        prepare_kernel,
        3,
        (idx, pairs, pair_count, embed, valid),
        [jax.ShapeDtypeStruct((8,), jnp.int32), bf16(HALF)],
    )
    qa = over_edge(first)
    x, second = call(
        normalize_kernel, 1, (table, embed), [bf16(2 * BLOCK + TILE), bf16(HALF)], flops=pair
    )
    sib = to_sibling(x)
    dens, acc = call(own_kernel, 1, (table, x), state, flops=4 * pair)
    dens, acc, second = lax.optimization_barrier((dens, acc, second))
    qb = over_edge(second)
    third, dens_a = call(
        third_kernel, 1, (table, qa, x, sib), [bf16(HALF), f32(HALF, LANES)], flops=2 * pair
    )
    dens, acc, third = lax.optimization_barrier((dens, acc, third))
    qc = over_edge(third)
    fa = to_sibling(qa)
    dens, acc = call(
        sibling_kernel, 1, (table, x, sib, dens, acc), state, {3: 0, 4: 1}, flops=4 * pair
    )
    fourth, _ = call(
        fourth_kernel,
        1,
        (table, qb, x, sib, dens_a),
        [bf16(HALF + TILE), f32(HALF, LANES)],
        flops=2 * pair,
    )
    dens, acc, fourth = lax.optimization_barrier((dens, acc, fourth))
    qd = over_edge(fourth)
    fb = to_sibling(qb)

    def near(s, *refs):
        near_kernel(s, n, *refs)

    dens, acc = call(
        near, 1, (table, x, sib, qa, qb, fa, fb, dens, acc), state, {7: 0, 8: 1}, flops=3 * pair
    )
    dens, acc = call(
        far_kernel, 1, (table, x, qa, qc, dens, acc), state, {4: 0, 5: 1}, flops=pair
    )
    logs, sums, _, _ = call(
        last_kernel,
        1,
        (table, x, qa, qd, dens, acc),
        [f32(2 * BLOCK // LANES, LANES), bf16(2 * BLOCK)] + state,
        {4: 2, 5: 3},
        flops=pair,
    )
    return logs.reshape(-1), sums


def solution(mesh):
    both = ("groups", "cluster")
    return jax.shard_map(
        per_device,
        mesh=mesh,
        in_specs=(P(both, None), P(both), P(both, None), P(both)),
        out_specs=(P(both), P(both, None)),
        check_vma=False,
    )
```

```python
import functools

import jax
import jax.numpy as jnp
from jax import lax
from jax.experimental import pallas as pl
from jax.experimental.pallas import tpu as pltpu
from jax.sharding import PartitionSpec as P

BLOCK = 512
HALF = BLOCK // 2
TILE = 16
LANES = 128
MARK = 100.0
SHARPNESS = 8.0
LOG2E = 1.4426950408889634

IDX, PAR, V0, V1, E0, E1, C0, C1 = range(8)

VM = pl.BlockSpec(memory_space=pltpu.VMEM)
SM = pl.BlockSpec(memory_space=pltpu.SMEM)
HB = pl.BlockSpec(memory_space=pltpu.HBM)


def iota(shape, dim):
    return lax.broadcasted_iota(jnp.int32, shape, dim)


def normalized(rows):
    wide = rows.astype(jnp.float32)
    scale = lax.rsqrt(jnp.mean(wide * wide, axis=-1, keepdims=True) + 1e-06)
    return wide * scale


def marked(rows, count):
    mark = jnp.where(iota(rows.shape, 1) == 0, MARK, 0.0)
    return jnp.where(iota(rows.shape, 0) < count, rows, mark).astype(jnp.bfloat16)


def real_rows(ref, start, rows):
    head = ref[pl.ds(start, rows), 0:LANES].astype(jnp.float32)
    real = jnp.logical_and(iota(head.shape, 1) == 0, head < 0.5 * MARK)
    return jnp.sum(jnp.where(real, 1.0, 0.0)).astype(jnp.int32)


def at(block):
    return pl.multiple_of(block * BLOCK, BLOCK)


def kernel_tile(left, right, count):
    gram = lax.dot_general(
        left, right, (((1,), (1,)), ((), ())), preferred_element_type=jnp.float32
    )
    scale = SHARPNESS * LOG2E / left.shape[1]
    kern = jnp.exp2(gram * scale - SHARPNESS * LOG2E)
    return jnp.where(iota(kern.shape, 1) < count, kern, 0.0)


def folded(kern):
    return functools.reduce(
        jnp.add, [kern[:, c : c + LANES] for c in range(0, kern.shape[1], LANES)]
    )


def terms(left, right, count):
    kern = kernel_tile(left, right, count)
    sums = jnp.dot(kern.astype(jnp.bfloat16), right, preferred_element_type=jnp.float32)
    return folded(kern), sums


def add_terms(x_ref, row, right, count, dens_ref, acc_ref):
    dens, sums = terms(x_ref[pl.ds(row, BLOCK), :], right, count)
    dens_ref[pl.ds(row, BLOCK), :] += dens
    acc_ref[pl.ds(row, BLOCK), :] += sums


def sibling_links(s, sib_ref):
    tile = sib_ref[pl.ds(2 * BLOCK, TILE), 0:LANES].astype(jnp.float32)
    lane = iota(tile.shape, 1)
    inner = jnp.max(jnp.where(lane == 0, tile, 0.0)) > 0.5
    outer = jnp.max(jnp.where(lane == 1, tile, 0.0)) > 0.5
    return inner, outer


def joined(s, outer):
    return jnp.where(s[PAR] == 1, outer.astype(jnp.int32), s[E1]) == 1


def first_kernel(idx_ref, embed_ref, first_ref, rows_ref, sems):
    near = at(idx_ref[0] % 2)
    part = HALF // 2
    copies = [
        pltpu.make_async_copy(
            embed_ref.at[pl.ds(near + p * part, part), :],
            rows_ref.at[pl.ds(p * part, part), :],
            sems.at[p],
        )
        for p in range(2)
    ]
    for copy in copies:
        copy.start()
    for p, copy in enumerate(copies):
        copy.wait()
        rows = slice(p * part, (p + 1) * part)
        first_ref[rows, :] = normalized(rows_ref[rows, :]).astype(jnp.bfloat16)


def normalize_kernel(
    idx_ref,
    pairs_hbm,
    count_ref,
    valid_hbm,
    embed_ref,
    s,
    x_ref,
    second_ref,
    rows_ref,
    valid_ref,
    pairs_ref,
    sems,
):
    small = [(pairs_hbm, pairs_ref), (valid_hbm, valid_ref)]
    small = [pltpu.make_async_copy(a, b, sems.at[4 + p]) for p, (a, b) in enumerate(small)]
    for copy in small:
        copy.start()
    copies = [
        pltpu.make_async_copy(
            embed_ref.at[pl.ds(p * HALF, HALF), :],
            rows_ref.at[pl.ds(p * HALF, HALF), :],
            sems.at[p],
        )
        for p in range(4)
    ]
    for copy in copies:
        copy.start()
    for copy in small:
        copy.wait()
    idx = idx_ref[0]
    counts = [jnp.int32(0), jnp.int32(0)]
    for slot in range(pairs_ref.shape[1]):
        live = slot < count_ref[0]
        for b in range(2):
            hit = jnp.logical_and(live, pairs_ref[0, slot] == idx * 2 + b)
            counts[b] = counts[b] + hit.astype(jnp.int32)
    per = valid_ref.shape[0] // 2
    reals = [
        jnp.sum(valid_ref[b * per : (b + 1) * per, :].astype(jnp.float32)).astype(jnp.int32)
        for b in range(2)
    ]
    links = [(c >= 2).astype(jnp.int32) for c in counts]
    s[IDX] = idx
    s[PAR] = idx % 2
    for b in range(2):
        s[V0 + b] = reals[b]
        s[E0 + b] = links[b]
        s[C0 + b] = counts[b]
    lane = iota((TILE, x_ref.shape[1]), 1)
    flags = jnp.where(
        lane == 0,
        links[0].astype(jnp.float32),
        jnp.where(lane == 1, links[1].astype(jnp.float32), 0.0),
    )
    x_ref[2 * BLOCK :, :] = flags.astype(jnp.bfloat16)
    for p, copy in enumerate(copies):
        copy.wait()
        rows = slice(p * HALF, (p + 1) * HALF)
        count = reals[p // 2] - (p % 2) * HALF
        x_ref[rows, :] = marked(normalized(rows_ref[rows, :]), count)
    near = idx % 2
    real = jnp.where(near == 1, reals[1], reals[0])
    apart = jnp.logical_and(near == 1, links[1] == 0)
    rows = x_ref[pl.ds(at(near) + HALF, HALF), :].astype(jnp.float32)
    lane, row = iota(rows.shape, 1), iota(rows.shape, 0)
    rows = jnp.where(apart, jnp.where(lane == 0, 2.0 * MARK, 0.0), rows)
    said = jnp.minimum(real, HALF).astype(jnp.float32) / LANES
    tell = jnp.logical_and(jnp.logical_and(row == HALF - 1, lane == 1), real < BLOCK)
    second_ref[...] = jnp.where(tell, said, rows).astype(jnp.bfloat16)


def near_rows(qb_ref):
    tail = qb_ref[HALF - TILE :, 0:LANES].astype(jnp.float32)
    lane, row = iota(tail.shape, 1), iota(tail.shape, 0)
    last = row == TILE - 1
    mark = jnp.max(jnp.where(jnp.logical_and(last, lane == 0), tail, -MARK))
    said = jnp.sum(jnp.where(jnp.logical_and(last, lane == 1), tail, 0.0)) * LANES
    first = jnp.where(mark < 0.5 * MARK, HALF, said.astype(jnp.int32))
    return mark < 1.5 * MARK, first, real_rows(qb_ref, 0, HALF)


def own_kernel(s, x_ref, dens_ref, acc_ref):
    for b in range(2):
        rows = x_ref[b * BLOCK : (b + 1) * BLOCK, :]
        dens, sums = terms(rows, rows, s[V0 + b])
        dens_ref[b * BLOCK : (b + 1) * BLOCK, :] = dens
        acc_ref[b * BLOCK : (b + 1) * BLOCK, :] = sums


def cross_kernel(s, x_ref, dens_in, acc_in, dens_ref, acc_ref):
    @pl.when(s[E0] == 1)
    def _():
        for b in range(2):
            other = x_ref[(1 - b) * BLOCK : (2 - b) * BLOCK, :]
            add_terms(x_ref, b * BLOCK, other, s[V0 + 1 - b], dens_ref, acc_ref)


def sibling_kernel(s, x_ref, sib_ref, dens_in, acc_in, dens_ref, acc_ref):
    inner, outer = sibling_links(s, sib_ref)
    near, far = at(s[PAR]), at(1 - s[PAR])
    meet = joined(s, outer)

    def column(start, use):
        @pl.when(use)
        def _():
            count = real_rows(sib_ref, start, BLOCK)
            right = sib_ref[pl.ds(start, BLOCK), :]
            add_terms(x_ref, far, right, count, dens_ref, acc_ref)

            @pl.when(s[E0] == 1)
            def _():
                add_terms(x_ref, near, right, count, dens_ref, acc_ref)

    column(near, meet)
    column(far, jnp.logical_and(meet, inner))


def partial_sums(s, half, q_ref, x_ref, sib_ref, out_ref, dens_ref):
    inner, outer = sibling_links(s, sib_ref)
    near, far = at(s[PAR]), at(1 - s[PAR])
    sums_go = jnp.where(s[PAR] == 1, s[C1] == 2, s[C0] == 3)

    @pl.when(sums_go)
    def _():
        left = q_ref[...]
        count = jnp.where(s[PAR] == 1, s[V0], s[V1]) * s[E0]
        dens, sums = terms(left, x_ref[pl.ds(far, BLOCK), :], count)
        use = jnp.logical_and(s[E0] == 1, joined(s, outer))
        count = jnp.where(use, real_rows(sib_ref, near, BLOCK), 0)
        more_dens, more_sums = terms(left, sib_ref[pl.ds(near, BLOCK), :], count)
        dens_ref[...] = dens + more_dens
        out_ref[0:HALF, :] = (sums + more_sums).astype(jnp.bfloat16)

    @pl.when(jnp.logical_not(sums_go))
    def _():
        dens_ref[...] = jnp.zeros_like(dens_ref)
        keep = jnp.logical_and(s[E0] == 1, jnp.logical_or(s[PAR] == 0, s[E1] == 1))
        rows = x_ref[pl.ds(far + half * HALF, HALF), :].astype(jnp.float32)
        out_ref[0:HALF, :] = marked(rows, jnp.where(keep, BLOCK, 0))


def along_lanes(dens):
    return jnp.sum(dens.T, axis=0, keepdims=True)


def third_kernel(s, q_ref, x_ref, sib_ref, out_ref, dens_ref):
    partial_sums(s, 0, q_ref, x_ref, sib_ref, out_ref, dens_ref)


def fourth_kernel(s, q_ref, x_ref, sib_ref, dens_a_ref, out_ref, dens_ref):
    partial_sums(s, 1, q_ref, x_ref, sib_ref, out_ref, dens_ref)
    width = out_ref.shape[1]
    both = [along_lanes(dens_a_ref[...]), along_lanes(dens_ref[...])]
    row = jnp.concatenate(both + [jnp.zeros((1, width - BLOCK), jnp.float32)], axis=1)
    place = iota((TILE, width), 0)
    tile = jnp.zeros((TILE, width), jnp.float32)
    for piece in range(3):
        rounded = row.astype(jnp.bfloat16).astype(jnp.float32)
        tile = jnp.where(place == piece, rounded, tile)
        row = row - rounded
    out_ref[HALF:, :] = tile.astype(jnp.bfloat16)


def across(s, qb_ref):
    joined_below, _, _ = near_rows(qb_ref)
    below = jnp.logical_and(s[IDX] > 0, joined_below)
    return jnp.where(s[PAR] == 1, s[E1], below.astype(jnp.int32)) == 1


def near_kernel(s, x_ref, sib_ref, qa_ref, qb_ref, fa_ref, fb_ref, dens_in, acc_in, dens_ref, acc_ref):
    near, far = at(s[PAR]), at(1 - s[PAR])

    @pl.when(across(s, qb_ref))
    def _():
        _, *counts = near_rows(qb_ref)
        for ref, count in zip((qa_ref, qb_ref), counts):
            add_terms(x_ref, near, ref[...], count, dens_ref, acc_ref)

        @pl.when(s[E0] == 1)
        def _():
            for ref, count in zip((qa_ref, qb_ref), counts):
                add_terms(x_ref, far, ref[...], count, dens_ref, acc_ref)

    inner, outer = sibling_links(s, sib_ref)
    below, *counts = near_rows(fb_ref)
    below = jnp.logical_and(s[IDX] > 1, below)
    beyond = jnp.where(s[PAR] == 1, below.astype(jnp.int32), outer.astype(jnp.int32)) == 1
    reached = jnp.logical_and(jnp.logical_and(joined(s, outer), inner), beyond)

    @pl.when(reached)
    def _():
        for ref, count in zip((fa_ref, fb_ref), counts):
            add_terms(x_ref, far, ref[...], count, dens_ref, acc_ref)


def what_came(s, qb_ref):
    linked = across(s, qb_ref)
    upper, lone = s[PAR] == 1, s[E0] == 0
    sums = jnp.where(upper, s[C1] == 4, jnp.logical_and(linked, lone))
    rows = jnp.where(upper, s[C1] == 3, jnp.logical_and(linked, jnp.logical_not(lone)))
    return sums, rows


def far_kernel(s, x_ref, qb_ref, q_ref, dens_in, acc_in, dens_ref, acc_ref):
    near, far = at(s[PAR]), at(1 - s[PAR])
    sums_came, rows_came = what_came(s, qb_ref)
    count = real_rows(q_ref, 0, HALF)

    @pl.when(sums_came)
    def _():
        acc_ref[pl.ds(near, HALF), :] += q_ref[...].astype(jnp.float32)

    @pl.when(jnp.logical_and(rows_came, count > 0))
    def _():
        add_terms(x_ref, near, q_ref[...], count, dens_ref, acc_ref)

        @pl.when(s[E0] == 1)
        def _():
            add_terms(x_ref, far, q_ref[...], count, dens_ref, acc_ref)


def last_kernel(
    s, x_ref, qb_ref, q_ref, dens_in, acc_in, log_ref, out_ref, dens_ref, acc_ref, rows_ref, sems
):
    near, far = at(s[PAR]), at(1 - s[PAR])
    sums_came, rows_came = what_came(s, qb_ref)
    count = real_rows(q_ref, 0, HALF)
    rows_came = jnp.logical_and(rows_came, count > 0)
    copies = []
    for which, row in enumerate((far, near)):
        use = jnp.logical_and(rows_came, s[E0] == 1) if which == 0 else rows_came

        @pl.when(use)
        def _():
            add_terms(x_ref, row, q_ref[0:HALF, :], count, dens_ref, acc_ref)

        if which == 1:

            @pl.when(sums_came)
            def _():
                acc_ref[pl.ds(near + HALF, HALF), :] += q_ref[0:HALF, :].astype(jnp.float32)

        real = jnp.where(s[PAR] == which, s[V1], s[V0])
        sums = acc_ref[pl.ds(row, BLOCK), :]
        kept = jnp.where(iota(sums.shape, 0) < real, sums, 0.0).astype(jnp.bfloat16)
        rows_ref[pl.ds(row, BLOCK), :] = kept
        place = pl.ds(row, BLOCK)
        copy = pltpu.make_async_copy(rows_ref.at[place, :], out_ref.at[place, :], sems.at[which])
        copy.start()
        copies.append(copy)
    tile = q_ref[HALF:, :].astype(jnp.float32)
    came = jnp.sum(jnp.where(iota(tile.shape, 0) < 3, tile, 0.0), axis=0, keepdims=True)
    per = BLOCK // LANES
    for b in range(2):
        density = along_lanes(dens_ref[b * BLOCK : (b + 1) * BLOCK, :])
        use = jnp.logical_and(sums_came, s[PAR] == b)
        density = density + jnp.where(use, came[:, 0:BLOCK], 0.0)
        real = iota(density.shape, 1) < s[V0 + b]
        logs = jnp.where(real, jnp.log(jnp.where(real, density, 1.0)), 0.0)
        for part in range(per):
            piece = logs[:, part * LANES : (part + 1) * LANES]
            log_ref[b * per + part : b * per + part + 1, :] = piece
    for copy in copies:
        copy.wait()


def call(kernel, us, in_spaces, operands, outs, out_spaces="", aliases=None, scratch=()):
    spaces = {"s": SM, "v": VM, "h": HB}
    out_spaces = out_spaces or "v" * len(outs)
    return pl.pallas_call(
        kernel,
        in_specs=[spaces[c] for c in in_spaces],
        out_specs=[spaces[c] for c in out_spaces],
        out_shape=outs,
        input_output_aliases=aliases or {},
        scratch_shapes=list(scratch),
        compiler_params=pltpu.CompilerParams(vmem_limit_bytes=16 << 20),
        cost_estimate=pl.CostEstimate(flops=int(us * 1.15e9), bytes_accessed=1 << 10, transcendentals=0),
    )(
        *[
            pltpu.with_memory_space_constraint(x, pltpu.HBM) if c == "h" else x
            for c, x in zip(in_spaces, operands)
        ]
    )


def after(value, *others):
    return lax.optimization_barrier((value, *others))[0]


def per_device(embed, valid, pairs, pair_count):
    width = embed.shape[1]
    chips = lax.axis_size("cluster") // 2
    idx = lax.axis_index("cluster").astype(jnp.int32).reshape(1)
    inchip = [(2 * c + k, 2 * c + 1 - k) for c in range(chips) for k in range(2)]
    edges = [(2 * c + 1, 2 * c + 2) for c in range(chips - 1)]
    edges = edges + [(b, a) for a, b in edges]

    def over_edge(block):
        return lax.ppermute(block, "cluster", edges)

    def to_sibling(block):
        return lax.ppermute(block, "cluster", inchip)

    bf16 = lambda rows: jax.ShapeDtypeStruct((rows, width), jnp.bfloat16)
    f32 = lambda rows, cols: jax.ShapeDtypeStruct((rows, cols), jnp.float32)
    state = [f32(2 * BLOCK, LANES), f32(2 * BLOCK, width)]
    dma = lambda count: pltpu.SemaphoreType.DMA((count,))
    vmem = lambda rows: pltpu.VMEM((rows, width), jnp.bfloat16)

    (first,) = call(
        first_kernel, 6.0, "sh", (idx, embed), [bf16(HALF)], scratch=(vmem(HALF), dma(2))
    )
    qa = over_edge(first)
    table, x, second = call(
        normalize_kernel,
        14.0,
        "shshh",
        (after(idx, first), pairs.T, pair_count, valid.reshape(-1, LANES), embed),
        [jax.ShapeDtypeStruct((8,), jnp.int32), bf16(2 * BLOCK + TILE), bf16(HALF)],
        "svv",
        scratch=(
            vmem(2 * BLOCK),
            pltpu.VMEM((2 * BLOCK // LANES, LANES), jnp.int32),
            pltpu.SMEM(pairs.shape[::-1], jnp.int32),
            dma(6),
        ),
    )
    sib = to_sibling(x)
    dens, acc = call(own_kernel, 13.0, "sv", (table, x), state)
    dens, acc, second = lax.optimization_barrier((dens, acc, second))
    qb = over_edge(second)
    dens, acc = call(
        cross_kernel, 13.0, "svvv", (table, x, dens, acc), state, aliases={2: 0, 3: 1}
    )
    third, dens_a = call(
        third_kernel,
        10.0,
        "svvv",
        (table, qa, after(x, acc), sib),
        [bf16(HALF), f32(HALF, LANES)],
    )
    qc = over_edge(third)
    fa = to_sibling(after(qa, third))
    fourth, _ = call(
        fourth_kernel,
        10.0,
        "svvvv",
        (table, qb, x, sib, dens_a),
        [bf16(HALF + TILE), f32(HALF, LANES)],
    )
    dens, acc, fourth = lax.optimization_barrier((dens, acc, fourth))
    qd = over_edge(fourth)
    fb = to_sibling(after(qb, fourth))
    dens, acc = call(
        sibling_kernel, 15.0, "svvvv", (table, x, sib, dens, acc), state, aliases={3: 0, 4: 1}
    )
    dens, acc = call(
        near_kernel,
        15.0,
        "svvvvvvvv",
        (table, x, sib, qa, qb, fa, fb, dens, acc),
        state,
        aliases={7: 0, 8: 1},
    )
    dens, acc = call(
        far_kernel, 5.0, "svvvvv", (table, x, qb, qc, dens, acc), state, aliases={4: 0, 5: 1}
    )
    logs, sums, _, _ = call(
        last_kernel,
        5.0,
        "svvvvv",
        (table, x, qb, qd, dens, acc),
        [f32(2 * BLOCK // LANES, LANES), bf16(2 * BLOCK)] + state,
        "vhvv",
        aliases={4: 2, 5: 3},
        scratch=(vmem(2 * BLOCK), dma(2)),
    )
    return logs.reshape(-1), sums


def solution(mesh):
    both = ("groups", "cluster")
    return jax.shard_map(
        per_device,
        mesh=mesh,
        in_specs=(P(both, None), P(both), P(both, None), P(both)),
        out_specs=(P(both), P(both, None)),
        check_vma=False,
    )
```

```python
import functools

import jax
import jax.numpy as jnp
from jax import lax
from jax.experimental import pallas as pl
from jax.experimental.pallas import tpu as pltpu
from jax.sharding import PartitionSpec as P

BLOCK = 512
HALF = BLOCK // 2
TILE = 16
LANES = 128
MARK = 100.0
SHARPNESS = 8.0
LOG2E = 1.4426950408889634

IDX, PAR, V0, V1, E0, E1, C0, C1 = range(8)

VM = pl.BlockSpec(memory_space=pltpu.VMEM)
SM = pl.BlockSpec(memory_space=pltpu.SMEM)
HB = pl.BlockSpec(memory_space=pltpu.HBM)


def iota(shape, dim):
    return lax.broadcasted_iota(jnp.int32, shape, dim)


def normalized(rows):
    wide = rows.astype(jnp.float32)
    scale = lax.rsqrt(jnp.mean(wide * wide, axis=-1, keepdims=True) + 1e-06)
    return wide * scale


def marked(rows, count):
    mark = jnp.where(iota(rows.shape, 1) == 0, MARK, 0.0)
    return jnp.where(iota(rows.shape, 0) < count, rows, mark).astype(jnp.bfloat16)


def real_rows(ref, start, rows):
    head = ref[pl.ds(start, rows), 0:LANES].astype(jnp.float32)
    real = jnp.logical_and(iota(head.shape, 1) == 0, head < 0.5 * MARK)
    return jnp.sum(jnp.where(real, 1.0, 0.0)).astype(jnp.int32)


def at(block):
    return pl.multiple_of(block * BLOCK, BLOCK)


def kernel_tile(left, right, count):
    gram = lax.dot_general(
        left, right, (((1,), (1,)), ((), ())), preferred_element_type=jnp.float32
    )
    scale = SHARPNESS * LOG2E / left.shape[1]
    kern = jnp.exp2(gram * scale - SHARPNESS * LOG2E)
    return jnp.where(iota(kern.shape, 1) < count, kern, 0.0)


def folded(kern):
    return functools.reduce(
        jnp.add, [kern[:, c : c + LANES] for c in range(0, kern.shape[1], LANES)]
    )


def terms(left, right, count):
    kern = kernel_tile(left, right, count)
    sums = jnp.dot(kern.astype(jnp.bfloat16), right, preferred_element_type=jnp.float32)
    return folded(kern), sums


def add_terms(x_ref, starts, rights, dens_ref, acc_ref):
    kerns = [
        [kernel_tile(x_ref[pl.ds(start, BLOCK), :], right, count) for right, count in rights]
        for start in starts
    ]
    for start, row in zip(starts, kerns):
        place = pl.ds(start, BLOCK)
        dens_ref[place, :] += functools.reduce(jnp.add, [folded(kern) for kern in row])
        sums = [
            jnp.dot(kern.astype(jnp.bfloat16), right, preferred_element_type=jnp.float32)
            for kern, (right, _) in zip(row, rights)
        ]
        acc_ref[place, :] += functools.reduce(jnp.add, sums)


def add_linked(s, start, other, x_ref, rights, dens_ref, acc_ref):
    @pl.when(s[E0] == 1)
    def _():
        add_terms(x_ref, (start, other), rights, dens_ref, acc_ref)

    @pl.when(s[E0] == 0)
    def _():
        add_terms(x_ref, (start,), rights, dens_ref, acc_ref)


def sibling_links(s, sib_ref):
    tile = sib_ref[pl.ds(2 * BLOCK, TILE), 0:LANES].astype(jnp.float32)
    lane = iota(tile.shape, 1)
    inner = jnp.max(jnp.where(lane == 0, tile, 0.0)) > 0.5
    outer = jnp.max(jnp.where(lane == 1, tile, 0.0)) > 0.5
    return inner, outer


def joined(s, outer):
    return jnp.where(s[PAR] == 1, outer.astype(jnp.int32), s[E1]) == 1


def first_kernel(idx_ref, valid_hbm, embed_ref, first_ref, rows_ref, valid_ref, sems):
    near = idx_ref[0] % 2
    rows = pltpu.make_async_copy(embed_ref.at[pl.ds(at(near), HALF), :], rows_ref, sems.at[0])
    flags = pltpu.make_async_copy(valid_hbm, valid_ref, sems.at[1])
    rows.start()
    flags.start()
    flags.wait()
    place = iota(valid_ref.shape, 0) // (valid_ref.shape[0] // 2)
    real = jnp.sum(jnp.where(place == near, valid_ref[...], 0).astype(jnp.float32))
    rows.wait()
    first_ref[...] = marked(normalized(rows_ref[...]), real.astype(jnp.int32))


def normalize_kernel(
    idx_ref, pairs_hbm, count_ref, valid_hbm, embed_ref, s, x_ref, second_ref,
    rows_ref, valid_ref, pairs_ref, sems
):
    small = [(pairs_hbm, pairs_ref), (valid_hbm, valid_ref)]
    small = [pltpu.make_async_copy(a, b, sems.at[4 + p]) for p, (a, b) in enumerate(small)]
    copies = [
        pltpu.make_async_copy(
            embed_ref.at[pl.ds(p * HALF, HALF), :],
            rows_ref.at[pl.ds(p * HALF, HALF), :],
            sems.at[p],
        )
        for p in range(4)
    ]
    for copy in small + copies:
        copy.start()
    for copy in small:
        copy.wait()
    idx = idx_ref[0]
    counts = [jnp.int32(0), jnp.int32(0)]
    for slot in range(pairs_ref.shape[1]):
        live = slot < count_ref[0]
        for b in range(2):
            hit = jnp.logical_and(live, pairs_ref[0, slot] == idx * 2 + b)
            counts[b] = counts[b] + hit.astype(jnp.int32)
    per = valid_ref.shape[0] // 2
    reals = [
        jnp.sum(valid_ref[b * per : (b + 1) * per, :].astype(jnp.float32)).astype(jnp.int32)
        for b in range(2)
    ]
    links = [(c >= 2).astype(jnp.int32) for c in counts]
    s[IDX] = idx
    s[PAR] = idx % 2
    for b in range(2):
        s[V0 + b] = reals[b]
        s[E0 + b] = links[b]
        s[C0 + b] = counts[b]
    lane = iota((TILE, x_ref.shape[1]), 1)
    flags = jnp.where(
        lane == 0,
        links[0].astype(jnp.float32),
        jnp.where(lane == 1, links[1].astype(jnp.float32), 0.0),
    )
    x_ref[2 * BLOCK :, :] = flags.astype(jnp.bfloat16)
    for p, copy in enumerate(copies):
        copy.wait()
        rows = slice(p * HALF, (p + 1) * HALF)
        count = reals[p // 2] - (p % 2) * HALF
        x_ref[rows, :] = marked(normalized(rows_ref[rows, :]), count)
    apart = jnp.logical_and(idx % 2 == 1, links[1] == 0)
    rows = x_ref[pl.ds(at(idx % 2) + HALF, HALF), :].astype(jnp.float32)
    mark = jnp.where(iota(rows.shape, 1) == 0, 2.0 * MARK, 0.0)
    second_ref[...] = jnp.where(apart, mark, rows).astype(jnp.bfloat16)


def own_kernel(s, x_ref, dens_ref, acc_ref):
    for b in range(2):
        rows = x_ref[b * BLOCK : (b + 1) * BLOCK, :]
        dens, sums = terms(rows, rows, s[V0 + b])
        dens_ref[b * BLOCK : (b + 1) * BLOCK, :] = dens
        acc_ref[b * BLOCK : (b + 1) * BLOCK, :] = sums

    @pl.when(s[E0] == 1)
    def _():
        for b in range(2):
            other = x_ref[(1 - b) * BLOCK : (2 - b) * BLOCK, :]
            add_terms(x_ref, (b * BLOCK,), [(other, s[V0 + 1 - b])], dens_ref, acc_ref)


def add_sibling(s, start, use, x_ref, sib_ref, dens_ref, acc_ref):
    @pl.when(use)
    def _():
        count = real_rows(sib_ref, start, BLOCK)
        rights = [(sib_ref[pl.ds(start, BLOCK), :], count)]
        add_linked(s, at(1 - s[PAR]), at(s[PAR]), x_ref, rights, dens_ref, acc_ref)


def beside_kernel(s, x_ref, sib_ref, dens_in, acc_in, dens_ref, acc_ref):
    inner, outer = sibling_links(s, sib_ref)
    add_sibling(s, at(s[PAR]), joined(s, outer), x_ref, sib_ref, dens_ref, acc_ref)


def not_apart(qb_ref):
    head = qb_ref[0:TILE, 0:LANES].astype(jnp.float32)
    first = jnp.logical_and(iota(head.shape, 0) == 0, iota(head.shape, 1) == 0)
    return jnp.sum(jnp.where(first, head, 0.0)) < 1.5 * MARK


def across(s, qb_ref):
    below = jnp.logical_and(s[IDX] > 0, not_apart(qb_ref))
    return jnp.where(s[PAR] == 1, s[E1], below.astype(jnp.int32)) == 1


def middle_kernel(s, x_ref, sib_ref, qa_ref, dens_in, acc_in, dens_ref, acc_ref):
    inner, outer = sibling_links(s, sib_ref)
    near, far = at(s[PAR]), at(1 - s[PAR])
    use = jnp.logical_and(joined(s, outer), inner)
    add_sibling(s, far, use, x_ref, sib_ref, dens_ref, acc_ref)

    @pl.when(jnp.logical_and(s[PAR] == 1, s[E1] == 1))
    def _():
        rights = [(qa_ref[...], real_rows(qa_ref, 0, HALF))]
        add_linked(s, near, far, x_ref, rights, dens_ref, acc_ref)


def partial_sums(s, half, q_ref, x_ref, sib_ref, out_ref, dens_ref):
    inner, outer = sibling_links(s, sib_ref)
    near, far = at(s[PAR]), at(1 - s[PAR])
    sums_go = jnp.where(s[PAR] == 1, s[C1] == 2, s[C0] == 3)

    @pl.when(sums_go)
    def _():
        left = q_ref[...]
        count = jnp.where(s[PAR] == 1, s[V0], s[V1]) * s[E0]
        dens, sums = terms(left, x_ref[pl.ds(far, BLOCK), :], count)
        use = jnp.logical_and(s[E0] == 1, joined(s, outer))
        count = jnp.where(use, real_rows(sib_ref, near, BLOCK), 0)
        more_dens, more_sums = terms(left, sib_ref[pl.ds(near, BLOCK), :], count)
        dens_ref[...] = dens + more_dens
        out_ref[0:HALF, :] = (sums + more_sums).astype(jnp.bfloat16)

    @pl.when(jnp.logical_not(sums_go))
    def _():
        dens_ref[...] = jnp.zeros_like(dens_ref)
        keep = jnp.logical_and(s[E0] == 1, jnp.logical_or(s[PAR] == 0, s[E1] == 1))
        rows = x_ref[pl.ds(far + half * HALF, HALF), :].astype(jnp.float32)
        out_ref[0:HALF, :] = marked(rows, jnp.where(keep, BLOCK, 0))


def along_lanes(dens):
    return jnp.sum(dens.T, axis=0, keepdims=True)


def third_kernel(s, q_ref, x_ref, sib_ref, out_ref, dens_ref):
    partial_sums(s, 0, q_ref, x_ref, sib_ref, out_ref, dens_ref)


def fourth_kernel(s, q_ref, x_ref, sib_ref, dens_a_ref, out_ref, dens_ref):
    partial_sums(s, 1, q_ref, x_ref, sib_ref, out_ref, dens_ref)
    width = out_ref.shape[1]
    both = [along_lanes(dens_a_ref[...]), along_lanes(dens_ref[...])]
    row = jnp.concatenate(both + [jnp.zeros((1, width - BLOCK), jnp.float32)], axis=1)
    place = iota((TILE, width), 0)
    tile = jnp.zeros((TILE, width), jnp.float32)
    for piece in range(3):
        rounded = row.astype(jnp.bfloat16).astype(jnp.float32)
        tile = jnp.where(place == piece, rounded, tile)
        row = row - rounded
    out_ref[HALF:, :] = tile.astype(jnp.bfloat16)


def outer_kernel(s, x_ref, qa_ref, qb_ref, dens_in, acc_in, dens_ref, acc_ref):
    near, far = at(s[PAR]), at(1 - s[PAR])
    linked = across(s, qb_ref)
    rights = [(ref[...], real_rows(ref, 0, HALF)) for ref in (qa_ref, qb_ref)]

    @pl.when(jnp.logical_and(linked, s[PAR] == 0))
    def _():
        add_linked(s, near, far, x_ref, rights, dens_ref, acc_ref)

    @pl.when(jnp.logical_and(linked, jnp.logical_and(s[PAR] == 1, rights[1][1] > 0)))
    def _():
        add_linked(s, near, far, x_ref, rights[1:], dens_ref, acc_ref)


def forward_kernel(s, x_ref, sib_ref, fa_ref, fb_ref, dens_in, acc_in, dens_ref, acc_ref):
    far = at(1 - s[PAR])
    inner, outer = sibling_links(s, sib_ref)
    below = jnp.logical_and(s[IDX] > 1, not_apart(fb_ref))
    beyond = jnp.where(s[PAR] == 1, below.astype(jnp.int32), outer.astype(jnp.int32)) == 1

    @pl.when(jnp.logical_and(jnp.logical_and(joined(s, outer), inner), beyond))
    def _():
        rights = [(ref[...], real_rows(ref, 0, HALF)) for ref in (fa_ref, fb_ref)]
        add_terms(x_ref, (far,), rights, dens_ref, acc_ref)


def what_came(s, qb_ref):
    linked = across(s, qb_ref)
    upper, lone = s[PAR] == 1, s[E0] == 0
    sums = jnp.where(upper, s[C1] == 4, jnp.logical_and(linked, lone))
    rows = jnp.where(upper, s[C1] == 3, jnp.logical_and(linked, jnp.logical_not(lone)))
    return sums, rows


def logs_of(density, real):
    use = iota(density.shape, 1) < real
    return jnp.where(use, jnp.log(jnp.where(use, density, 1.0)), 0.0)


def put_logs(log_ref, block, logs):
    per = BLOCK // LANES
    for part in range(per):
        log_ref[pl.ds(block * per + part, 1), :] = logs[:, part * LANES : (part + 1) * LANES]


def finished(sums, start, real):
    return jnp.where(iota(sums.shape, 0) + start < real, sums, 0.0).astype(jnp.bfloat16)


def far_kernel(
    s, x_ref, qb_ref, q_ref, dens_in, acc_in, log_ref, out_ref, dens_ref, acc_ref, rows_ref, sems
):
    near, far = at(s[PAR]), at(1 - s[PAR])
    sums_came, rows_came = what_came(s, qb_ref)

    @pl.when(rows_came)
    def _():
        count = real_rows(q_ref, 0, HALF)
        add_linked(s, near, far, x_ref, [(q_ref[...], count)], dens_ref, acc_ref)

    @pl.when(jnp.logical_not(rows_came))
    def _():
        @pl.when(sums_came)
        def _():
            acc_ref[pl.ds(near, HALF), :] += q_ref[...].astype(jnp.float32)

        copies = []
        for b in range(2):
            rows = pl.ds(b * BLOCK, BLOCK)
            rows_ref[rows, :] = finished(acc_ref[rows, :], 0, s[V0 + b])
            copy = pltpu.make_async_copy(rows_ref.at[rows, :], out_ref.at[rows, :], sems.at[b])
            copy.start()
            copies.append(copy)
        for b in range(2):
            density = along_lanes(dens_ref[b * BLOCK : (b + 1) * BLOCK, :])
            put_logs(log_ref, b, logs_of(density, s[V0 + b]))
        for copy in copies:
            copy.wait()


def last_kernel(
    s, x_ref, qb_ref, q_ref, dens_ref, acc_ref, log_in, out_in, log_ref, out_ref,
    rows_ref, place_ref, sems
):
    sums_came, rows_came = what_came(s, qb_ref)
    log_copy = pltpu.make_async_copy(place_ref, log_ref, sems.at[4])

    @pl.when(rows_came)
    def _():
        count = real_rows(q_ref, 0, HALF)
        right = q_ref[0:HALF, :]
        kerns = []
        for b in range(2):
            left = x_ref[b * BLOCK : (b + 1) * BLOCK, :]
            kerns.append(kernel_tile(left, right, jnp.where(s[PAR] == b, count, count * s[E0])))
        copies = []
        for b in range(2):
            for half in range(2):
                rows = pl.ds(b * BLOCK + half * HALF, HALF)
                kern = kerns[b][half * HALF : (half + 1) * HALF].astype(jnp.bfloat16)
                sums = acc_ref[rows, :] + jnp.dot(kern, right, preferred_element_type=jnp.float32)
                rows_ref[rows, :] = finished(sums, half * HALF, s[V0 + b])
                copy = pltpu.make_async_copy(
                    rows_ref.at[rows, :], out_ref.at[rows, :], sems.at[2 * b + half]
                )
                copy.start()
                copies.append(copy)
            if b == 0:
                for c in range(2):
                    density = dens_ref[c * BLOCK : (c + 1) * BLOCK, :] + folded(kerns[c])
                    put_logs(place_ref, c, logs_of(along_lanes(density), s[V0 + c]))
                log_copy.start()
                copies.append(log_copy)
        for copy in copies:
            copy.wait()

    @pl.when(jnp.logical_not(rows_came))
    def _():
        place_ref[...] = log_in[...]

        @pl.when(sums_came)
        def _():
            near = at(s[PAR])
            real = jnp.where(s[PAR] == 1, s[V1], s[V0])
            rows = pl.ds(near + HALF, HALF)
            sums = acc_ref[rows, :] + q_ref[0:HALF, :].astype(jnp.float32)
            rows_ref[rows, :] = finished(sums, HALF, real)
            copy = pltpu.make_async_copy(rows_ref.at[rows, :], out_ref.at[rows, :], sems.at[0])
            copy.start()
            tile = q_ref[HALF:, :].astype(jnp.float32)
            came = jnp.sum(jnp.where(iota(tile.shape, 0) < 3, tile, 0.0), axis=0, keepdims=True)
            density = along_lanes(dens_ref[pl.ds(near, BLOCK), :]) + came[:, 0:BLOCK]
            put_logs(place_ref, s[PAR], logs_of(density, real))
            log_copy.start()
            copy.wait()
            log_copy.wait()

        @pl.when(jnp.logical_not(sums_came))
        def _():
            log_copy.start()
            log_copy.wait()


def call(kernel, us, in_spaces, operands, outs, out_spaces="", aliases=None, scratch=()):
    spaces = {"s": SM, "v": VM, "h": HB}
    out_spaces = out_spaces or "v" * len(outs)
    return pl.pallas_call(
        kernel,
        in_specs=[spaces[c] for c in in_spaces],
        out_specs=[spaces[c] for c in out_spaces],
        out_shape=outs,
        input_output_aliases=aliases or {},
        scratch_shapes=list(scratch),
        compiler_params=pltpu.CompilerParams(vmem_limit_bytes=16 << 20),
        cost_estimate=pl.CostEstimate(flops=int(us * 1.15e9), bytes_accessed=1 << 10, transcendentals=0),
    )(
        *[
            pltpu.with_memory_space_constraint(x, pltpu.HBM) if c == "h" else x
            for c, x in zip(in_spaces, operands)
        ]
    )


def after(value, *others):
    return lax.optimization_barrier((value, *others))[0]


def per_device(embed, valid, pairs, pair_count):
    width = embed.shape[1]
    chips = lax.axis_size("cluster") // 2
    idx = lax.axis_index("cluster").astype(jnp.int32).reshape(1)
    inchip = [(2 * c + k, 2 * c + 1 - k) for c in range(chips) for k in range(2)]
    edges = [(2 * c + 1, 2 * c + 2) for c in range(chips - 1)]
    edges = edges + [(b, a) for a, b in edges]

    def over_edge(block):
        return lax.ppermute(block, "cluster", edges)

    def to_sibling(block):
        return lax.ppermute(block, "cluster", inchip)

    bf16 = lambda rows: jax.ShapeDtypeStruct((rows, width), jnp.bfloat16)
    f32 = lambda rows, cols: jax.ShapeDtypeStruct((rows, cols), jnp.float32)
    state = [f32(2 * BLOCK, LANES), f32(2 * BLOCK, width)]
    dma = lambda count: pltpu.SemaphoreType.DMA((count,))
    vmem = lambda rows: pltpu.VMEM((rows, width), jnp.bfloat16)

    flags = valid.reshape(-1, LANES)
    (first,) = call(
        first_kernel,
        6.0,
        "shh",
        (idx, flags, embed),
        [bf16(HALF)],
        scratch=(vmem(HALF), pltpu.VMEM(flags.shape, jnp.int32), dma(2)),
    )
    qa = over_edge(first)
    table, x, second = call(
        normalize_kernel,
        14.0,
        "shshh",
        (after(idx, first), pairs.T, pair_count, flags, embed),
        [jax.ShapeDtypeStruct((8,), jnp.int32), bf16(2 * BLOCK + TILE), bf16(HALF)],
        "svv",
        scratch=(
            vmem(2 * BLOCK),
            pltpu.VMEM(flags.shape, jnp.int32),
            pltpu.SMEM(pairs.shape[::-1], jnp.int32),
            dma(6),
        ),
    )
    qb = over_edge(second)
    sib = to_sibling(x)
    dens, acc = call(own_kernel, 60, "sv", (table, x), state)
    dens, acc = call(
        beside_kernel, 13.0, "svvvv", (table, x, sib, dens, acc), state, aliases={3: 0, 4: 1}
    )
    third, dens_a = call(
        third_kernel,
        10.0,
        "svvv",
        (table, qa, after(x, acc), sib),
        [bf16(HALF), f32(HALF, LANES)],
    )
    qc = over_edge(third)
    dens, acc, _ = lax.optimization_barrier((dens, acc, third))
    dens, acc = call(
        middle_kernel, 15.0, "svvvvv", (table, x, sib, qa, dens, acc), state, aliases={4: 0, 5: 1}
    )
    fourth, _ = call(
        fourth_kernel,
        10.0,
        "svvvv",
        (table, qb, after(x, acc), sib, dens_a),
        [bf16(HALF + TILE), f32(HALF, LANES)],
    )
    dens, acc, fourth = lax.optimization_barrier((dens, acc, fourth))
    qd = over_edge(fourth)
    fa = to_sibling(after(qa, fourth))
    fb = to_sibling(after(qb, fourth))
    dens, acc = call(
        outer_kernel, 15.0, "svvvvv", (table, x, qa, qb, dens, acc), state, aliases={4: 0, 5: 1}
    )
    dens, acc = call(
        forward_kernel,
        15.0,
        "svvvvvv",
        (table, x, sib, fa, fb, dens, acc),
        state,
        aliases={5: 0, 6: 1},
    )
    logs, sums, dens, acc = call(
        far_kernel,
        5.0,
        "svvvvv",
        (table, x, qb, qc, dens, acc),
        [f32(2 * BLOCK // LANES, LANES), bf16(2 * BLOCK)] + state,
        "vhvv",
        aliases={4: 2, 5: 3},
        scratch=(vmem(2 * BLOCK), dma(2)),
    )
    logs, sums = call(
        last_kernel,
        5.0,
        "svvvvvvh",
        (table, x, qb, qd, dens, acc, logs, sums),
        [f32(2 * BLOCK // LANES, LANES), bf16(2 * BLOCK)],
        "hh",
        aliases={7: 1},
        scratch=(
            vmem(2 * BLOCK),
            pltpu.VMEM((2 * BLOCK // LANES, LANES), jnp.float32),
            dma(5),
        ),
    )
    return logs.reshape(-1), sums


def solution(mesh):
    both = ("groups", "cluster")
    return jax.shard_map(
        per_device,
        mesh=mesh,
        in_specs=(P(both, None), P(both), P(both, None), P(both)),
        out_specs=(P(both), P(both, None)),
        check_vma=False,
    )
```

```python
import functools

import jax
import jax.numpy as jnp
from jax import lax
from jax.experimental import pallas as pl
from jax.experimental.pallas import tpu as pltpu
from jax.sharding import PartitionSpec as P

BLOCK = 512
HALF = BLOCK // 2
TILE = 16
LANES = 128
MARK = 100.0
SHARPNESS = 8.0
LOG2E = 1.4426950408889634

IDX, PAR, V0, V1, E0, E1, C0, C1 = range(8)

VM = pl.BlockSpec(memory_space=pltpu.VMEM)
SM = pl.BlockSpec(memory_space=pltpu.SMEM)
HB = pl.BlockSpec(memory_space=pltpu.HBM)


def iota(shape, dim):
    return lax.broadcasted_iota(jnp.int32, shape, dim)


def normalized(rows):
    wide = rows.astype(jnp.float32)
    scale = lax.rsqrt(jnp.mean(wide * wide, axis=-1, keepdims=True) + 1e-06)
    return wide * scale


def marked(rows, count):
    mark = jnp.where(iota(rows.shape, 1) == 0, MARK, 0.0)
    return jnp.where(iota(rows.shape, 0) < count, rows, mark).astype(jnp.bfloat16)


def real_rows(ref, start, rows):
    head = ref[pl.ds(start, rows), 0:LANES].astype(jnp.float32)
    real = jnp.logical_and(iota(head.shape, 1) == 0, head < 0.5 * MARK)
    return jnp.sum(jnp.where(real, 1.0, 0.0)).astype(jnp.int32)


def at(block):
    return pl.multiple_of(block * BLOCK, BLOCK)


def kernel_tile(left, right, count):
    gram = lax.dot_general(
        left, right, (((1,), (1,)), ((), ())), preferred_element_type=jnp.float32
    )
    scale = SHARPNESS * LOG2E / left.shape[1]
    kern = jnp.exp2(gram * scale - SHARPNESS * LOG2E)
    return jnp.where(iota(kern.shape, 1) < count, kern, 0.0)


def folded(kern):
    return functools.reduce(
        jnp.add, [kern[:, c : c + LANES] for c in range(0, kern.shape[1], LANES)]
    )


def terms(left, right, count):
    kern = kernel_tile(left, right, count)
    sums = jnp.dot(kern.astype(jnp.bfloat16), right, preferred_element_type=jnp.float32)
    return folded(kern), sums


def add_terms(x_ref, starts, rights, dens_ref, acc_ref):
    kerns = [
        [kernel_tile(x_ref[pl.ds(start, BLOCK), :], right, count) for right, count in rights]
        for start in starts
    ]
    for start, row in zip(starts, kerns):
        place = pl.ds(start, BLOCK)
        dens_ref[place, :] += functools.reduce(jnp.add, [folded(kern) for kern in row])
        sums = [
            jnp.dot(kern.astype(jnp.bfloat16), right, preferred_element_type=jnp.float32)
            for kern, (right, _) in zip(row, rights)
        ]
        acc_ref[place, :] += functools.reduce(jnp.add, sums)


def add_linked(s, start, other, x_ref, rights, dens_ref, acc_ref):
    @pl.when(s[E0] == 1)
    def _():
        add_terms(x_ref, (start, other), rights, dens_ref, acc_ref)

    @pl.when(s[E0] == 0)
    def _():
        add_terms(x_ref, (start,), rights, dens_ref, acc_ref)


def sibling_links(s, sib_ref):
    tile = sib_ref[pl.ds(2 * BLOCK, TILE), 0:LANES].astype(jnp.float32)
    lane = iota(tile.shape, 1)
    inner = jnp.max(jnp.where(lane == 0, tile, 0.0)) > 0.5
    outer = jnp.max(jnp.where(lane == 1, tile, 0.0)) > 0.5
    return inner, outer


def joined(s, outer):
    return jnp.where(s[PAR] == 1, outer.astype(jnp.int32), s[E1]) == 1


def first_kernel(idx_ref, valid_hbm, embed_ref, first_ref, rows_ref, valid_ref, sems):
    near = idx_ref[0] % 2
    rows = pltpu.make_async_copy(embed_ref.at[pl.ds(at(near), HALF), :], rows_ref, sems.at[0])
    flags = pltpu.make_async_copy(valid_hbm, valid_ref, sems.at[1])
    rows.start()
    flags.start()
    flags.wait()
    place = iota(valid_ref.shape, 0) // (valid_ref.shape[0] // 2)
    real = jnp.sum(jnp.where(place == near, valid_ref[...], 0).astype(jnp.float32))
    rows.wait()
    first_ref[...] = marked(normalized(rows_ref[...]), real.astype(jnp.int32))


def normalize_kernel(
    idx_ref, pairs_hbm, count_ref, valid_hbm, embed_ref, s, x_ref, second_ref,
    rows_ref, valid_ref, pairs_ref, sems
):
    small = [(pairs_hbm, pairs_ref), (valid_hbm, valid_ref)]
    small = [pltpu.make_async_copy(a, b, sems.at[4 + p]) for p, (a, b) in enumerate(small)]
    copies = [
        pltpu.make_async_copy(
            embed_ref.at[pl.ds(p * HALF, HALF), :],
            rows_ref.at[pl.ds(p * HALF, HALF), :],
            sems.at[p],
        )
        for p in range(4)
    ]
    for copy in small + copies:
        copy.start()
    for copy in small:
        copy.wait()
    idx = idx_ref[0]
    counts = [jnp.int32(0), jnp.int32(0)]
    for slot in range(pairs_ref.shape[1]):
        live = slot < count_ref[0]
        for b in range(2):
            hit = jnp.logical_and(live, pairs_ref[0, slot] == idx * 2 + b)
            counts[b] = counts[b] + hit.astype(jnp.int32)
    per = valid_ref.shape[0] // 2
    reals = [
        jnp.sum(valid_ref[b * per : (b + 1) * per, :].astype(jnp.float32)).astype(jnp.int32)
        for b in range(2)
    ]
    links = [(c >= 2).astype(jnp.int32) for c in counts]
    s[IDX] = idx
    s[PAR] = idx % 2
    for b in range(2):
        s[V0 + b] = reals[b]
        s[E0 + b] = links[b]
        s[C0 + b] = counts[b]
    lane = iota((TILE, x_ref.shape[1]), 1)
    flags = jnp.where(
        lane == 0,
        links[0].astype(jnp.float32),
        jnp.where(lane == 1, links[1].astype(jnp.float32), 0.0),
    )
    x_ref[2 * BLOCK :, :] = flags.astype(jnp.bfloat16)
    for p, copy in enumerate(copies):
        copy.wait()
        rows = slice(p * HALF, (p + 1) * HALF)
        count = reals[p // 2] - (p % 2) * HALF
        x_ref[rows, :] = marked(normalized(rows_ref[rows, :]), count)
    apart = jnp.logical_and(idx % 2 == 1, links[1] == 0)
    rows = x_ref[pl.ds(at(idx % 2) + HALF, HALF), :].astype(jnp.float32)
    mark = jnp.where(iota(rows.shape, 1) == 0, 2.0 * MARK, 0.0)
    second_ref[...] = jnp.where(apart, mark, rows).astype(jnp.bfloat16)


def own_kernel(s, x_ref, dens_ref, acc_ref):
    for b in range(2):
        rows = x_ref[b * BLOCK : (b + 1) * BLOCK, :]
        dens, sums = terms(rows, rows, s[V0 + b])
        dens_ref[b * BLOCK : (b + 1) * BLOCK, :] = dens
        acc_ref[b * BLOCK : (b + 1) * BLOCK, :] = sums

    @pl.when(s[E0] == 1)
    def _():
        for b in range(2):
            other = x_ref[(1 - b) * BLOCK : (2 - b) * BLOCK, :]
            add_terms(x_ref, (b * BLOCK,), [(other, s[V0 + 1 - b])], dens_ref, acc_ref)


def add_sibling(s, start, use, x_ref, sib_ref, dens_ref, acc_ref):
    @pl.when(use)
    def _():
        count = real_rows(sib_ref, start, BLOCK)
        rights = [(sib_ref[pl.ds(start, BLOCK), :], count)]
        add_linked(s, at(1 - s[PAR]), at(s[PAR]), x_ref, rights, dens_ref, acc_ref)


def beside_kernel(s, x_ref, sib_ref, dens_in, acc_in, third_ref, fourth_ref, dens_ref, acc_ref):
    far = at(1 - s[PAR])
    keep = jnp.logical_and(s[E0] == 1, jnp.logical_or(s[PAR] == 0, s[E1] == 1))
    for half, ref in enumerate((third_ref, fourth_ref)):
        rows = x_ref[pl.ds(far + half * HALF, HALF), :].astype(jnp.float32)
        ref[0:HALF, :] = marked(rows, jnp.where(keep, BLOCK, 0))
    inner, outer = sibling_links(s, sib_ref)
    add_sibling(s, at(s[PAR]), joined(s, outer), x_ref, sib_ref, dens_ref, acc_ref)


def not_apart(qb_ref):
    head = qb_ref[0:TILE, 0:LANES].astype(jnp.float32)
    first = jnp.logical_and(iota(head.shape, 0) == 0, iota(head.shape, 1) == 0)
    return jnp.sum(jnp.where(first, head, 0.0)) < 1.5 * MARK


def across(s, qb_ref):
    below = jnp.logical_and(s[IDX] > 0, not_apart(qb_ref))
    return jnp.where(s[PAR] == 1, s[E1], below.astype(jnp.int32)) == 1


def middle_kernel(s, x_ref, sib_ref, qa_ref, dens_in, acc_in, dens_ref, acc_ref):
    inner, outer = sibling_links(s, sib_ref)
    near, far = at(s[PAR]), at(1 - s[PAR])
    use = jnp.logical_and(joined(s, outer), inner)
    add_sibling(s, far, use, x_ref, sib_ref, dens_ref, acc_ref)

    @pl.when(jnp.logical_and(s[PAR] == 1, s[E1] == 1))
    def _():
        rights = [(qa_ref[...], real_rows(qa_ref, 0, HALF))]
        add_linked(s, near, far, x_ref, rights, dens_ref, acc_ref)


def sums_go(s):
    return jnp.where(s[PAR] == 1, s[C1] == 2, s[C0] == 3)


def partial_sums(s, q_ref, x_ref, sib_ref, out_ref, dens_ref):
    _, outer = sibling_links(s, sib_ref)
    near, far = at(s[PAR]), at(1 - s[PAR])
    left = q_ref[...]
    count = jnp.where(s[PAR] == 1, s[V0], s[V1]) * s[E0]
    use = jnp.logical_and(s[E0] == 1, joined(s, outer))
    beside = jnp.where(use, real_rows(sib_ref, near, BLOCK), 0)
    rights = [(x_ref[pl.ds(far, BLOCK), :], count), (sib_ref[pl.ds(near, BLOCK), :], beside)]
    kerns = [kernel_tile(left, right, count) for right, count in rights]
    sums = [
        jnp.dot(kern.astype(jnp.bfloat16), right, preferred_element_type=jnp.float32)
        for kern, (right, _) in zip(kerns, rights)
    ]
    dens_ref[...] = folded(kerns[0]) + folded(kerns[1])
    out_ref[0:HALF, :] = (sums[0] + sums[1]).astype(jnp.bfloat16)


def along_lanes(dens):
    return jnp.sum(dens.T, axis=0, keepdims=True)


def third_kernel(s, q_ref, x_ref, sib_ref, out_in, out_ref, dens_ref):
    @pl.when(sums_go(s))
    def _():
        partial_sums(s, q_ref, x_ref, sib_ref, out_ref, dens_ref)


def fourth_kernel(s, q_ref, x_ref, sib_ref, dens_a_ref, out_in, out_ref, dens_ref):
    @pl.when(sums_go(s))
    def _():
        partial_sums(s, q_ref, x_ref, sib_ref, out_ref, dens_ref)
        width = out_ref.shape[1]
        both = [along_lanes(dens_a_ref[...]), along_lanes(dens_ref[...])]
        row = jnp.concatenate(both + [jnp.zeros((1, width - BLOCK), jnp.float32)], axis=1)
        place = iota((TILE, width), 0)
        tile = jnp.zeros((TILE, width), jnp.float32)
        for piece in range(3):
            rounded = row.astype(jnp.bfloat16).astype(jnp.float32)
            tile = jnp.where(place == piece, rounded, tile)
            row = row - rounded
        out_ref[HALF:, :] = tile.astype(jnp.bfloat16)


def outer_kernel(s, x_ref, qa_ref, qb_ref, dens_in, acc_in, came, dens_ref, acc_ref):
    near, far = at(s[PAR]), at(1 - s[PAR])
    linked = across(s, qb_ref)
    upper, lone = s[PAR] == 1, s[E0] == 0
    sums = jnp.where(upper, s[C1] == 4, jnp.logical_and(linked, lone))
    rows = jnp.where(upper, s[C1] == 3, jnp.logical_and(linked, jnp.logical_not(lone)))
    came[0] = sums.astype(jnp.int32)
    came[1] = rows.astype(jnp.int32)
    rights = [(ref[...], real_rows(ref, 0, HALF)) for ref in (qa_ref, qb_ref)]

    @pl.when(jnp.logical_and(linked, s[PAR] == 0))
    def _():
        add_linked(s, near, far, x_ref, rights, dens_ref, acc_ref)

    @pl.when(jnp.logical_and(linked, jnp.logical_and(s[PAR] == 1, rights[1][1] > 0)))
    def _():
        add_linked(s, near, far, x_ref, rights[1:], dens_ref, acc_ref)


def forward_kernel(s, x_ref, sib_ref, fa_ref, fb_ref, dens_in, acc_in, dens_ref, acc_ref):
    far = at(1 - s[PAR])
    inner, outer = sibling_links(s, sib_ref)
    below = jnp.logical_and(s[IDX] > 1, not_apart(fb_ref))
    beyond = jnp.where(s[PAR] == 1, below.astype(jnp.int32), outer.astype(jnp.int32)) == 1

    @pl.when(jnp.logical_and(jnp.logical_and(joined(s, outer), inner), beyond))
    def _():
        rights = [(ref[...], real_rows(ref, 0, HALF)) for ref in (fa_ref, fb_ref)]
        add_terms(x_ref, (far,), rights, dens_ref, acc_ref)


def logs_of(density, real):
    use = iota(density.shape, 1) < real
    return jnp.where(use, jnp.log(jnp.where(use, density, 1.0)), 0.0)


def put_logs(log_ref, block, logs):
    per = BLOCK // LANES
    for part in range(per):
        log_ref[pl.ds(block * per + part, 1), :] = logs[:, part * LANES : (part + 1) * LANES]


def finished(sums, start, real):
    return jnp.where(iota(sums.shape, 0) + start < real, sums, 0.0).astype(jnp.bfloat16)


def far_kernel(
    s, came, x_ref, q_ref, dens_in, acc_in, log_out, out_ref, dens_ref, acc_ref,
    rows_ref, log_ref, sems
):
    near, far = at(s[PAR]), at(1 - s[PAR])

    @pl.when(came[1] == 1)
    def _():
        count = real_rows(q_ref, 0, HALF)
        add_linked(s, near, far, x_ref, [(q_ref[...], count)], dens_ref, acc_ref)

    @pl.when(came[1] == 0)
    def _():
        @pl.when(came[0] == 1)
        def _():
            acc_ref[pl.ds(near, HALF), :] += q_ref[...].astype(jnp.float32)

        copies = []
        for b in range(2):
            rows = pl.ds(b * BLOCK, BLOCK)
            rows_ref[rows, :] = finished(acc_ref[rows, :], 0, s[V0 + b])
            copy = pltpu.make_async_copy(rows_ref.at[rows, :], out_ref.at[rows, :], sems.at[b])
            copy.start()
            copies.append(copy)
        for b in range(2):
            density = along_lanes(dens_ref[b * BLOCK : (b + 1) * BLOCK, :])
            put_logs(log_ref, b, logs_of(density, s[V0 + b]))
        copy = pltpu.make_async_copy(log_ref, log_out, sems.at[2])
        copy.start()
        for copy in copies + [copy]:
            copy.wait()


def last_kernel(
    s, came, x_ref, q_ref, dens_ref, acc_ref, log_in, out_in, log_out, out_ref,
    rows_ref, log_ref, sems
):
    log_copy = pltpu.make_async_copy(log_ref, log_out, sems.at[4])

    @pl.when(came[1] == 1)
    def _():
        count = real_rows(q_ref, 0, HALF)
        right = q_ref[0:HALF, :]
        kerns = []
        for b in range(2):
            left = x_ref[b * BLOCK : (b + 1) * BLOCK, :]
            kerns.append(kernel_tile(left, right, jnp.where(s[PAR] == b, count, count * s[E0])))
        copies = []
        for b in range(2):
            for half in range(2):
                rows = pl.ds(b * BLOCK + half * HALF, HALF)
                kern = kerns[b][half * HALF : (half + 1) * HALF].astype(jnp.bfloat16)
                sums = acc_ref[rows, :] + jnp.dot(kern, right, preferred_element_type=jnp.float32)
                rows_ref[rows, :] = finished(sums, half * HALF, s[V0 + b])
                copy = pltpu.make_async_copy(
                    rows_ref.at[rows, :], out_ref.at[rows, :], sems.at[2 * b + half]
                )
                copy.start()
                copies.append(copy)
            if b == 0:
                for c in range(2):
                    density = dens_ref[c * BLOCK : (c + 1) * BLOCK, :] + folded(kerns[c])
                    put_logs(log_ref, c, logs_of(along_lanes(density), s[V0 + c]))
                log_copy.start()
                copies.append(log_copy)
        for copy in copies:
            copy.wait()

    @pl.when(came[0] == 1)
    def _():
        near = at(s[PAR])
        real = jnp.where(s[PAR] == 1, s[V1], s[V0])
        rows = pl.ds(near + HALF, HALF)
        sums = acc_ref[rows, :] + q_ref[0:HALF, :].astype(jnp.float32)
        rows_ref[rows, :] = finished(sums, HALF, real)
        copy = pltpu.make_async_copy(rows_ref.at[rows, :], out_ref.at[rows, :], sems.at[0])
        copy.start()
        for b in range(2):
            tile = q_ref[HALF:, :].astype(jnp.float32)
            pieces = jnp.where(iota(tile.shape, 0) < 3, tile, 0.0)
            more = jnp.sum(pieces, axis=0, keepdims=True)[:, 0:BLOCK]
            density = along_lanes(dens_ref[b * BLOCK : (b + 1) * BLOCK, :])
            density = density + jnp.where(s[PAR] == b, more, 0.0)
            put_logs(log_ref, b, logs_of(density, s[V0 + b]))
        log_copy.start()
        copy.wait()
        log_copy.wait()


def call(kernel, us, in_spaces, operands, outs, out_spaces="", aliases=None, scratch=()):
    spaces = {"s": SM, "v": VM, "h": HB}
    out_spaces = out_spaces or "v" * len(outs)
    return pl.pallas_call(
        kernel,
        in_specs=[spaces[c] for c in in_spaces],
        out_specs=[spaces[c] for c in out_spaces],
        out_shape=outs,
        input_output_aliases=aliases or {},
        scratch_shapes=list(scratch),
        compiler_params=pltpu.CompilerParams(vmem_limit_bytes=16 << 20),
        cost_estimate=pl.CostEstimate(flops=int(us * 1.15e9), bytes_accessed=1 << 10, transcendentals=0),
    )(
        *[
            pltpu.with_memory_space_constraint(x, pltpu.HBM) if c == "h" else x
            for c, x in zip(in_spaces, operands)
        ]
    )


def after(value, *others):
    return lax.optimization_barrier((value, *others))[0]


def per_device(embed, valid, pairs, pair_count):
    width = embed.shape[1]
    chips = lax.axis_size("cluster") // 2
    idx = lax.axis_index("cluster").astype(jnp.int32).reshape(1)
    inchip = [(2 * c + k, 2 * c + 1 - k) for c in range(chips) for k in range(2)]
    edges = [(2 * c + 1, 2 * c + 2) for c in range(chips - 1)]
    edges = edges + [(b, a) for a, b in edges]

    def over_edge(block):
        return lax.ppermute(block, "cluster", edges)

    def to_sibling(block):
        return lax.ppermute(block, "cluster", inchip)

    bf16 = lambda rows: jax.ShapeDtypeStruct((rows, width), jnp.bfloat16)
    f32 = lambda rows, cols: jax.ShapeDtypeStruct((rows, cols), jnp.float32)
    state = [f32(2 * BLOCK, LANES), f32(2 * BLOCK, width)]
    dma = lambda count: pltpu.SemaphoreType.DMA((count,))
    vmem = lambda rows: pltpu.VMEM((rows, width), jnp.bfloat16)

    flags = valid.reshape(-1, LANES)
    (first,) = call(
        first_kernel,
        6.0,
        "shh",
        (idx, flags, embed),
        [bf16(HALF)],
        scratch=(vmem(HALF), pltpu.VMEM(flags.shape, jnp.int32), dma(2)),
    )
    qa = over_edge(first)
    table, x, second = call(
        normalize_kernel,
        14.0,
        "shshh",
        (after(idx, first), pairs.T, pair_count, flags, embed),
        [jax.ShapeDtypeStruct((8,), jnp.int32), bf16(2 * BLOCK + TILE), bf16(HALF)],
        "svv",
        scratch=(
            vmem(2 * BLOCK),
            pltpu.VMEM(flags.shape, jnp.int32),
            pltpu.SMEM(pairs.shape[::-1], jnp.int32),
            dma(6),
        ),
    )
    qb = over_edge(second)
    sib = to_sibling(x)
    dens, acc = call(own_kernel, 60, "sv", (table, x), state)
    third, fourth, dens, acc = call(
        beside_kernel,
        13.0,
        "svvvv",
        (table, x, sib, dens, acc),
        [bf16(HALF), bf16(HALF + TILE)] + state,
        aliases={3: 2, 4: 3},
    )
    third, dens_a = call(
        third_kernel,
        10.0,
        "svvvv",
        (table, qa, x, sib, third),
        [bf16(HALF), f32(HALF, LANES)],
        aliases={4: 0},
    )
    qc = over_edge(third)
    dens, acc, _ = lax.optimization_barrier((dens, acc, third))
    dens, acc = call(
        middle_kernel, 15.0, "svvvvv", (table, x, sib, qa, dens, acc), state, aliases={4: 0, 5: 1}
    )
    (fourth,) = call(
        fourth_kernel,
        10.0,
        "svvvvv",
        (table, qb, after(x, acc), sib, dens_a, fourth),
        [bf16(HALF + TILE)],
        aliases={5: 0},
        scratch=(pltpu.VMEM((HALF, LANES), jnp.float32),),
    )
    dens, acc, fourth = lax.optimization_barrier((dens, acc, fourth))
    qd = over_edge(fourth)
    fa = to_sibling(after(qa, fourth))
    fb = to_sibling(after(qb, fourth))
    came, dens, acc = call(
        outer_kernel,
        15.0,
        "svvvvv",
        (table, x, qa, qb, dens, acc),
        [jax.ShapeDtypeStruct((2,), jnp.int32)] + state,
        "svv",
        aliases={4: 1, 5: 2},
    )
    dens, acc = call(
        forward_kernel,
        15.0,
        "svvvvvv",
        (table, x, sib, fa, fb, dens, acc),
        state,
        aliases={5: 0, 6: 1},
    )
    log_shape = f32(2 * BLOCK // LANES, LANES)
    logs, sums, dens, acc = call(
        far_kernel,
        5.0,
        "ssvvvv",
        (table, came, x, qc, dens, acc),
        [log_shape, bf16(2 * BLOCK)] + state,
        "hhvv",
        aliases={4: 2, 5: 3},
        scratch=(vmem(2 * BLOCK), pltpu.VMEM(log_shape.shape, jnp.float32), dma(3)),
    )
    logs, sums = call(
        last_kernel,
        5.0,
        "ssvvvvhh",
        (table, came, x, qd, dens, acc, logs, sums),
        [log_shape, bf16(2 * BLOCK)],
        "hh",
        aliases={6: 0, 7: 1},
        scratch=(vmem(2 * BLOCK), pltpu.VMEM(log_shape.shape, jnp.float32), dma(5)),
    )
    return logs.reshape(-1), sums


def solution(mesh):
    both = ("groups", "cluster")
    return jax.shard_map(
        per_device,
        mesh=mesh,
        in_specs=(P(both, None), P(both), P(both, None), P(both)),
        out_specs=(P(both), P(both, None)),
        check_vma=False,
    )
```

```python
import functools

import jax
import jax.numpy as jnp
from jax import lax
from jax.experimental import pallas as pl
from jax.experimental.pallas import tpu as pltpu
from jax.sharding import PartitionSpec as P

BLOCK = 512
HALF = BLOCK // 2
TILE = 16
LANES = 128
MARK = 100.0
SHARPNESS = 8.0
LOG2E = 1.4426950408889634

IDX, PAR, V0, V1, E0, E1, C0, C1 = range(8)

VM = pl.BlockSpec(memory_space=pltpu.VMEM)
SM = pl.BlockSpec(memory_space=pltpu.SMEM)
HB = pl.BlockSpec(memory_space=pltpu.HBM)


def iota(shape, dim):
    return lax.broadcasted_iota(jnp.int32, shape, dim)


def normalized(rows):
    wide = rows.astype(jnp.float32)
    scale = lax.rsqrt(jnp.mean(wide * wide, axis=-1, keepdims=True) + 1e-06)
    return wide * scale


def marked(rows, count):
    mark = jnp.where(iota(rows.shape, 1) == 0, MARK, 0.0)
    return jnp.where(iota(rows.shape, 0) < count, rows, mark).astype(jnp.bfloat16)


def real_rows(ref, start, rows):
    head = ref[pl.ds(start, rows), 0:LANES].astype(jnp.float32)
    real = jnp.logical_and(iota(head.shape, 1) == 0, head < 0.5 * MARK)
    return jnp.sum(jnp.where(real, 1.0, 0.0)).astype(jnp.int32)


def at(block):
    return pl.multiple_of(block * BLOCK, BLOCK)


def kernel_tile(left, right, count):
    gram = lax.dot_general(
        left, right, (((1,), (1,)), ((), ())), preferred_element_type=jnp.float32
    )
    scale = SHARPNESS * LOG2E / left.shape[1]
    kern = jnp.exp2(gram * scale - SHARPNESS * LOG2E)
    return jnp.where(iota(kern.shape, 1) < count, kern, 0.0)


def folded(kern):
    return functools.reduce(
        jnp.add, [kern[:, c : c + LANES] for c in range(0, kern.shape[1], LANES)]
    )


def terms(left, right, count):
    kern = kernel_tile(left, right, count)
    sums = jnp.dot(kern.astype(jnp.bfloat16), right, preferred_element_type=jnp.float32)
    return folded(kern), sums


def add_terms(x_ref, starts, rights, dens_ref, acc_ref):
    kerns = [
        [kernel_tile(x_ref[pl.ds(start, BLOCK), :], right, count) for right, count in rights]
        for start in starts
    ]
    for start, row in zip(starts, kerns):
        place = pl.ds(start, BLOCK)
        dens_ref[place, :] += functools.reduce(jnp.add, [folded(kern) for kern in row])
        sums = [
            jnp.dot(kern.astype(jnp.bfloat16), right, preferred_element_type=jnp.float32)
            for kern, (right, _) in zip(row, rights)
        ]
        acc_ref[place, :] += functools.reduce(jnp.add, sums)


def add_linked(s, start, other, x_ref, rights, dens_ref, acc_ref):
    @pl.when(s[E0] == 1)
    def _():
        add_terms(x_ref, (start, other), rights, dens_ref, acc_ref)

    @pl.when(s[E0] == 0)
    def _():
        add_terms(x_ref, (start,), rights, dens_ref, acc_ref)


def sibling_links(s, sib_ref):
    tile = sib_ref[pl.ds(2 * BLOCK, TILE), 0:LANES].astype(jnp.float32)
    lane = iota(tile.shape, 1)
    inner = jnp.max(jnp.where(lane == 0, tile, 0.0)) > 0.5
    outer = jnp.max(jnp.where(lane == 1, tile, 0.0)) > 0.5
    return inner, outer


def joined(s, outer):
    return jnp.where(s[PAR] == 1, outer.astype(jnp.int32), s[E1]) == 1


def first_kernel(idx_ref, valid_hbm, embed_ref, first_ref, rows_ref, valid_ref, sems):
    near = idx_ref[0] % 2
    rows = pltpu.make_async_copy(embed_ref.at[pl.ds(at(near), HALF), :], rows_ref, sems.at[0])
    flags = pltpu.make_async_copy(valid_hbm, valid_ref, sems.at[1])
    rows.start()
    flags.start()
    flags.wait()
    place = iota(valid_ref.shape, 0) // (valid_ref.shape[0] // 2)
    real = jnp.sum(jnp.where(place == near, valid_ref[...], 0).astype(jnp.float32))
    rows.wait()
    first_ref[...] = marked(normalized(rows_ref[...]), real.astype(jnp.int32))


def normalize_kernel(
    idx_ref, pairs_hbm, count_ref, valid_hbm, embed_ref, s, x_ref, second_ref,
    rows_ref, valid_ref, pairs_ref, sems
):
    small = [(pairs_hbm, pairs_ref), (valid_hbm, valid_ref)]
    small = [pltpu.make_async_copy(a, b, sems.at[4 + p]) for p, (a, b) in enumerate(small)]
    copies = [
        pltpu.make_async_copy(
            embed_ref.at[pl.ds(p * HALF, HALF), :],
            rows_ref.at[pl.ds(p * HALF, HALF), :],
            sems.at[p],
        )
        for p in range(4)
    ]
    for copy in small + copies:
        copy.start()
    for copy in small:
        copy.wait()
    idx = idx_ref[0]
    counts = [jnp.int32(0), jnp.int32(0)]
    for slot in range(pairs_ref.shape[1]):
        live = slot < count_ref[0]
        for b in range(2):
            hit = jnp.logical_and(live, pairs_ref[0, slot] == idx * 2 + b)
            counts[b] = counts[b] + hit.astype(jnp.int32)
    per = valid_ref.shape[0] // 2
    reals = [
        jnp.sum(valid_ref[b * per : (b + 1) * per, :].astype(jnp.float32)).astype(jnp.int32)
        for b in range(2)
    ]
    links = [(c >= 2).astype(jnp.int32) for c in counts]
    s[IDX] = idx
    s[PAR] = idx % 2
    for b in range(2):
        s[V0 + b] = reals[b]
        s[E0 + b] = links[b]
        s[C0 + b] = counts[b]
    lane = iota((TILE, x_ref.shape[1]), 1)
    flags = jnp.where(
        lane == 0,
        links[0].astype(jnp.float32),
        jnp.where(lane == 1, links[1].astype(jnp.float32), 0.0),
    )
    x_ref[2 * BLOCK :, :] = flags.astype(jnp.bfloat16)
    for p, copy in enumerate(copies):
        copy.wait()
        rows = slice(p * HALF, (p + 1) * HALF)
        count = reals[p // 2] - (p % 2) * HALF
        x_ref[rows, :] = marked(normalized(rows_ref[rows, :]), count)
    apart = jnp.logical_and(idx % 2 == 1, links[1] == 0)
    rows = x_ref[pl.ds(at(idx % 2) + HALF, HALF), :].astype(jnp.float32)
    mark = jnp.where(iota(rows.shape, 1) == 0, 2.0 * MARK, 0.0)
    second_ref[...] = jnp.where(apart, mark, rows).astype(jnp.bfloat16)


def own_block(s, b, x_ref, dens_ref, acc_ref):
    rows = x_ref[b * BLOCK : (b + 1) * BLOCK, :]
    dens, sums = terms(rows, rows, s[V0 + b])
    dens_ref[b * BLOCK : (b + 1) * BLOCK, :] = dens
    acc_ref[b * BLOCK : (b + 1) * BLOCK, :] = sums


def own_kernel(s, x_ref, dens_ref, acc_ref):
    own_block(s, 0, x_ref, dens_ref, acc_ref)


def cross_kernel(s, x_ref, dens_in, acc_in, third_ref, fourth_ref, dens_ref, acc_ref):
    own_block(s, 1, x_ref, dens_ref, acc_ref)
    far = at(1 - s[PAR])
    keep = jnp.logical_and(s[E0] == 1, jnp.logical_or(s[PAR] == 0, s[E1] == 1))
    for half, ref in enumerate((third_ref, fourth_ref)):
        rows = x_ref[pl.ds(far + half * HALF, HALF), :].astype(jnp.float32)
        ref[0:HALF, :] = marked(rows, jnp.where(keep, BLOCK, 0))

    @pl.when(s[E0] == 1)
    def _():
        for b in range(2):
            other = x_ref[(1 - b) * BLOCK : (2 - b) * BLOCK, :]
            add_terms(x_ref, (b * BLOCK,), [(other, s[V0 + 1 - b])], dens_ref, acc_ref)


def add_sibling(s, start, use, x_ref, sib_ref, dens_ref, acc_ref):
    @pl.when(use)
    def _():
        count = real_rows(sib_ref, start, BLOCK)
        rights = [(sib_ref[pl.ds(start, BLOCK), :], count)]
        add_linked(s, at(1 - s[PAR]), at(s[PAR]), x_ref, rights, dens_ref, acc_ref)


def not_apart(qb_ref):
    head = qb_ref[0:TILE, 0:LANES].astype(jnp.float32)
    first = jnp.logical_and(iota(head.shape, 0) == 0, iota(head.shape, 1) == 0)
    return jnp.sum(jnp.where(first, head, 0.0)) < 1.5 * MARK


def across(s, qb_ref):
    below = jnp.logical_and(s[IDX] > 0, not_apart(qb_ref))
    return jnp.where(s[PAR] == 1, s[E1], below.astype(jnp.int32)) == 1


def middle_kernel(s, x_ref, sib_ref, qa_ref, dens_in, acc_in, dens_ref, acc_ref):
    inner, outer = sibling_links(s, sib_ref)
    near, far = at(s[PAR]), at(1 - s[PAR])
    meet = joined(s, outer)
    add_sibling(s, near, meet, x_ref, sib_ref, dens_ref, acc_ref)
    add_sibling(s, far, jnp.logical_and(meet, inner), x_ref, sib_ref, dens_ref, acc_ref)

    @pl.when(jnp.logical_and(s[PAR] == 1, s[E1] == 1))
    def _():
        rights = [(qa_ref[...], real_rows(qa_ref, 0, HALF))]
        add_linked(s, near, far, x_ref, rights, dens_ref, acc_ref)


def sums_go(s):
    return jnp.where(s[PAR] == 1, s[C1] == 2, s[C0] == 3)


def partial_sums(s, q_ref, x_ref, sib_ref, out_ref, dens_ref):
    _, outer = sibling_links(s, sib_ref)
    near, far = at(s[PAR]), at(1 - s[PAR])
    left = q_ref[...]
    count = jnp.where(s[PAR] == 1, s[V0], s[V1]) * s[E0]
    use = jnp.logical_and(s[E0] == 1, joined(s, outer))
    beside = jnp.where(use, real_rows(sib_ref, near, BLOCK), 0)
    rights = [(x_ref[pl.ds(far, BLOCK), :], count), (sib_ref[pl.ds(near, BLOCK), :], beside)]
    kerns = [kernel_tile(left, right, count) for right, count in rights]
    sums = [
        jnp.dot(kern.astype(jnp.bfloat16), right, preferred_element_type=jnp.float32)
        for kern, (right, _) in zip(kerns, rights)
    ]
    dens_ref[...] = folded(kerns[0]) + folded(kerns[1])
    out_ref[0:HALF, :] = (sums[0] + sums[1]).astype(jnp.bfloat16)


def along_lanes(dens):
    return jnp.sum(dens.T, axis=0, keepdims=True)


def third_kernel(s, q_ref, x_ref, sib_ref, out_in, out_ref, dens_ref):
    @pl.when(sums_go(s))
    def _():
        partial_sums(s, q_ref, x_ref, sib_ref, out_ref, dens_ref)


def fourth_kernel(s, q_ref, x_ref, sib_ref, dens_a_ref, out_in, out_ref, dens_ref):
    @pl.when(sums_go(s))
    def _():
        partial_sums(s, q_ref, x_ref, sib_ref, out_ref, dens_ref)
        width = out_ref.shape[1]
        both = [along_lanes(dens_a_ref[...]), along_lanes(dens_ref[...])]
        row = jnp.concatenate(both + [jnp.zeros((1, width - BLOCK), jnp.float32)], axis=1)
        place = iota((TILE, width), 0)
        tile = jnp.zeros((TILE, width), jnp.float32)
        for piece in range(3):
            rounded = row.astype(jnp.bfloat16).astype(jnp.float32)
            tile = jnp.where(place == piece, rounded, tile)
            row = row - rounded
        out_ref[HALF:, :] = tile.astype(jnp.bfloat16)


def outer_kernel(s, x_ref, qa_ref, qb_ref, dens_in, acc_in, came, dens_ref, acc_ref):
    near, far = at(s[PAR]), at(1 - s[PAR])
    linked = across(s, qb_ref)
    upper, lone = s[PAR] == 1, s[E0] == 0
    sums = jnp.where(upper, s[C1] == 4, jnp.logical_and(linked, lone))
    rows = jnp.where(upper, s[C1] == 3, jnp.logical_and(linked, jnp.logical_not(lone)))
    came[0] = sums.astype(jnp.int32)
    came[1] = rows.astype(jnp.int32)
    rights = [(ref[...], real_rows(ref, 0, HALF)) for ref in (qa_ref, qb_ref)]

    @pl.when(jnp.logical_and(linked, s[PAR] == 0))
    def _():
        add_linked(s, near, far, x_ref, rights, dens_ref, acc_ref)

    @pl.when(jnp.logical_and(linked, jnp.logical_and(s[PAR] == 1, rights[1][1] > 0)))
    def _():
        add_linked(s, near, far, x_ref, rights[1:], dens_ref, acc_ref)


def forward_kernel(s, x_ref, sib_ref, fa_ref, fb_ref, dens_in, acc_in, dens_ref, acc_ref):
    far = at(1 - s[PAR])
    inner, outer = sibling_links(s, sib_ref)
    below = jnp.logical_and(s[IDX] > 1, not_apart(fb_ref))
    beyond = jnp.where(s[PAR] == 1, below.astype(jnp.int32), outer.astype(jnp.int32)) == 1

    @pl.when(jnp.logical_and(jnp.logical_and(joined(s, outer), inner), beyond))
    def _():
        rights = [(ref[...], real_rows(ref, 0, HALF)) for ref in (fa_ref, fb_ref)]
        add_terms(x_ref, (far,), rights, dens_ref, acc_ref)


def logs_of(density, real):
    use = iota(density.shape, 1) < real
    return jnp.where(use, jnp.log(jnp.where(use, density, 1.0)), 0.0)


def put_logs(log_ref, block, logs):
    per = BLOCK // LANES
    for part in range(per):
        log_ref[pl.ds(block * per + part, 1), :] = logs[:, part * LANES : (part + 1) * LANES]


def finished(sums, start, real):
    return jnp.where(iota(sums.shape, 0) + start < real, sums, 0.0).astype(jnp.bfloat16)


def far_kernel(
    s, came, x_ref, q_ref, dens_in, acc_in, lanes_ref, log_out, out_ref, dens_ref, acc_ref,
    rows_ref, log_ref, sems
):
    near, far = at(s[PAR]), at(1 - s[PAR])

    @pl.when(came[1] == 1)
    def _():
        count = real_rows(q_ref, 0, HALF)
        add_linked(s, near, far, x_ref, [(q_ref[...], count)], dens_ref, acc_ref)

    @pl.when(came[1] == 0)
    def _():
        @pl.when(came[0] == 1)
        def _():
            acc_ref[pl.ds(near, HALF), :] += q_ref[...].astype(jnp.float32)

        copies = []
        for b in range(2):
            rows = pl.ds(b * BLOCK, BLOCK)
            rows_ref[rows, :] = finished(acc_ref[rows, :], 0, s[V0 + b])
            copy = pltpu.make_async_copy(rows_ref.at[rows, :], out_ref.at[rows, :], sems.at[b])
            copy.start()
            copies.append(copy)
        for b in range(2):
            density = along_lanes(dens_ref[b * BLOCK : (b + 1) * BLOCK, :])
            lanes_ref[b : b + 1, :] = density
            put_logs(log_ref, b, logs_of(density, s[V0 + b]))
        copy = pltpu.make_async_copy(log_ref, log_out, sems.at[2])
        copy.start()
        for copy in copies + [copy]:
            copy.wait()


def last_kernel(
    s, came, x_ref, q_ref, lanes_ref, dens_ref, acc_ref, log_in, out_in, log_out, out_ref,
    rows_ref, log_ref, sems
):
    log_copy = pltpu.make_async_copy(log_ref, log_out, sems.at[4])

    @pl.when(came[1] == 1)
    def _():
        count = real_rows(q_ref, 0, HALF)
        right = q_ref[0:HALF, :]
        kerns = []
        for b in range(2):
            left = x_ref[b * BLOCK : (b + 1) * BLOCK, :]
            kerns.append(kernel_tile(left, right, jnp.where(s[PAR] == b, count, count * s[E0])))
        copies = []
        for b in range(2):
            for half in range(2):
                rows = pl.ds(b * BLOCK + half * HALF, HALF)
                kern = kerns[b][half * HALF : (half + 1) * HALF].astype(jnp.bfloat16)
                sums = acc_ref[rows, :] + jnp.dot(kern, right, preferred_element_type=jnp.float32)
                rows_ref[rows, :] = finished(sums, half * HALF, s[V0 + b])
                copy = pltpu.make_async_copy(
                    rows_ref.at[rows, :], out_ref.at[rows, :], sems.at[2 * b + half]
                )
                copy.start()
                copies.append(copy)
            if b == 0:
                for c in range(2):
                    density = dens_ref[c * BLOCK : (c + 1) * BLOCK, :] + folded(kerns[c])
                    put_logs(log_ref, c, logs_of(along_lanes(density), s[V0 + c]))
                log_copy.start()
                copies.append(log_copy)
        for copy in copies:
            copy.wait()

    @pl.when(came[0] == 1)
    def _():
        near = at(s[PAR])
        real = jnp.where(s[PAR] == 1, s[V1], s[V0])
        rows = pl.ds(near + HALF, HALF)
        sums = acc_ref[rows, :] + q_ref[0:HALF, :].astype(jnp.float32)
        rows_ref[rows, :] = finished(sums, HALF, real)
        copy = pltpu.make_async_copy(rows_ref.at[rows, :], out_ref.at[rows, :], sems.at[0])
        copy.start()
        tile = q_ref[HALF:, :].astype(jnp.float32)
        pieces = jnp.where(iota(tile.shape, 0) < 3, tile, 0.0)
        more = jnp.sum(pieces, axis=0, keepdims=True)[:, 0:BLOCK]
        for b in range(2):
            density = lanes_ref[b : b + 1, :] + jnp.where(s[PAR] == b, more, 0.0)
            put_logs(log_ref, b, logs_of(density, s[V0 + b]))
        log_copy.start()
        copy.wait()
        log_copy.wait()


def call(kernel, us, in_spaces, operands, outs, out_spaces="", aliases=None, scratch=()):
    spaces = {"s": SM, "v": VM, "h": HB}
    out_spaces = out_spaces or "v" * len(outs)
    return pl.pallas_call(
        kernel,
        in_specs=[spaces[c] for c in in_spaces],
        out_specs=[spaces[c] for c in out_spaces],
        out_shape=outs,
        input_output_aliases=aliases or {},
        scratch_shapes=list(scratch),
        compiler_params=pltpu.CompilerParams(vmem_limit_bytes=16 << 20),
        cost_estimate=pl.CostEstimate(flops=int(us * 1.15e9), bytes_accessed=1 << 10, transcendentals=0),
    )(
        *[
            pltpu.with_memory_space_constraint(x, pltpu.HBM) if c == "h" else x
            for c, x in zip(in_spaces, operands)
        ]
    )


def after(value, *others):
    return lax.optimization_barrier((value, *others))[0]


def per_device(embed, valid, pairs, pair_count):
    width = embed.shape[1]
    chips = lax.axis_size("cluster") // 2
    idx = lax.axis_index("cluster").astype(jnp.int32).reshape(1)
    inchip = [(2 * c + k, 2 * c + 1 - k) for c in range(chips) for k in range(2)]
    edges = [(2 * c + 1, 2 * c + 2) for c in range(chips - 1)]
    edges = edges + [(b, a) for a, b in edges]

    def over_edge(block):
        return lax.ppermute(block, "cluster", edges)

    def to_sibling(block):
        return lax.ppermute(block, "cluster", inchip)

    bf16 = lambda rows: jax.ShapeDtypeStruct((rows, width), jnp.bfloat16)
    f32 = lambda rows, cols: jax.ShapeDtypeStruct((rows, cols), jnp.float32)
    state = [f32(2 * BLOCK, LANES), f32(2 * BLOCK, width)]
    dma = lambda count: pltpu.SemaphoreType.DMA((count,))
    vmem = lambda rows: pltpu.VMEM((rows, width), jnp.bfloat16)

    flags = valid.reshape(-1, LANES)
    (first,) = call(
        first_kernel,
        6.0,
        "shh",
        (idx, flags, embed),
        [bf16(HALF)],
        scratch=(vmem(HALF), pltpu.VMEM(flags.shape, jnp.int32), dma(2)),
    )
    qa = over_edge(first)
    table, x, second = call(
        normalize_kernel,
        14.0,
        "shshh",
        (after(idx, first), pairs.T, pair_count, flags, embed),
        [jax.ShapeDtypeStruct((8,), jnp.int32), bf16(2 * BLOCK + TILE), bf16(HALF)],
        "svv",
        scratch=(
            vmem(2 * BLOCK),
            pltpu.VMEM(flags.shape, jnp.int32),
            pltpu.SMEM(pairs.shape[::-1], jnp.int32),
            dma(6),
        ),
    )
    sib = to_sibling(x)
    dens, acc = call(own_kernel, 30.0, "sv", (table, x), state)
    dens, acc, second = lax.optimization_barrier((dens, acc, second))
    qb = over_edge(second)
    third, fourth, dens, acc = call(
        cross_kernel,
        13.0,
        "svvv",
        (table, x, dens, acc),
        [bf16(HALF), bf16(HALF + TILE)] + state,
        aliases={2: 2, 3: 3},
    )
    third, dens_a = call(
        third_kernel,
        10.0,
        "svvvv",
        (table, qa, x, sib, third),
        [bf16(HALF), f32(HALF, LANES)],
        aliases={4: 0},
    )
    qc = over_edge(third)
    dens, acc, _ = lax.optimization_barrier((dens, acc, third))
    dens, acc = call(
        middle_kernel, 15.0, "svvvvv", (table, x, sib, qa, dens, acc), state, aliases={4: 0, 5: 1}
    )
    (fourth,) = call(
        fourth_kernel,
        10.0,
        "svvvvv",
        (table, qb, after(x, acc), sib, dens_a, fourth),
        [bf16(HALF + TILE)],
        aliases={5: 0},
        scratch=(pltpu.VMEM((HALF, LANES), jnp.float32),),
    )
    dens, acc, fourth = lax.optimization_barrier((dens, acc, fourth))
    qd = over_edge(fourth)
    fa = to_sibling(after(qa, fourth))
    fb = to_sibling(after(qb, fourth))
    came, dens, acc = call(
        outer_kernel,
        15.0,
        "svvvvv",
        (table, x, qa, qb, dens, acc),
        [jax.ShapeDtypeStruct((2,), jnp.int32)] + state,
        "svv",
        aliases={4: 1, 5: 2},
    )
    dens, acc = call(
        forward_kernel,
        15.0,
        "svvvvvv",
        (table, x, sib, fa, fb, dens, acc),
        state,
        aliases={5: 0, 6: 1},
    )
    log_shape = f32(2 * BLOCK // LANES, LANES)
    lanes, logs, sums, dens, acc = call(
        far_kernel,
        5.0,
        "ssvvvv",
        (table, came, x, qc, dens, acc),
        [f32(8, BLOCK), log_shape, bf16(2 * BLOCK)] + state,
        "vhhvv",
        aliases={4: 3, 5: 4},
        scratch=(vmem(2 * BLOCK), pltpu.VMEM(log_shape.shape, jnp.float32), dma(3)),
    )
    logs, sums = call(
        last_kernel,
        5.0,
        "ssvvvvvhh",
        (table, came, x, qd, lanes, dens, acc, logs, sums),
        [log_shape, bf16(2 * BLOCK)],
        "hh",
        aliases={7: 0, 8: 1},
        scratch=(vmem(2 * BLOCK), pltpu.VMEM(log_shape.shape, jnp.float32), dma(5)),
    )
    return logs.reshape(-1), sums


def solution(mesh):
    both = ("groups", "cluster")
    return jax.shard_map(
        per_device,
        mesh=mesh,
        in_specs=(P(both, None), P(both), P(both, None), P(both)),
        out_specs=(P(both), P(both, None)),
        check_vma=False,
    )
```

```python
import functools

import jax
import jax.numpy as jnp
from jax import lax
from jax.experimental import pallas as pl
from jax.experimental.pallas import tpu as pltpu
from jax.sharding import PartitionSpec as P

BLOCK = 512
HALF = BLOCK // 2
TILE = 16
LANES = 128
MARK = 100.0
SHARPNESS = 8.0
LOG2E = 1.4426950408889634

IDX, PAR, V0, V1, E0, E1, C0, C1, SUMS, ROWS = range(10)

VM = pl.BlockSpec(memory_space=pltpu.VMEM)
SM = pl.BlockSpec(memory_space=pltpu.SMEM)
HB = pl.BlockSpec(memory_space=pltpu.HBM)


def iota(shape, dim):
    return lax.broadcasted_iota(jnp.int32, shape, dim)


def normalized(rows):
    wide = rows.astype(jnp.float32)
    scale = lax.rsqrt(jnp.mean(wide * wide, axis=-1, keepdims=True) + 1e-06)
    return wide * scale


def marked(rows, count):
    mark = jnp.where(iota(rows.shape, 1) == 0, MARK, 0.0)
    return jnp.where(iota(rows.shape, 0) < count, rows, mark).astype(jnp.bfloat16)


def real_rows(ref, start, rows):
    head = ref[pl.ds(start, rows), 0:LANES].astype(jnp.float32)
    real = jnp.logical_and(iota(head.shape, 1) == 0, head < 0.5 * MARK)
    return jnp.sum(jnp.where(real, 1.0, 0.0)).astype(jnp.int32)


def at(block):
    return pl.multiple_of(block * BLOCK, BLOCK)


def kernel_tile(left, right, count):
    gram = lax.dot_general(
        left, right, (((1,), (1,)), ((), ())), preferred_element_type=jnp.float32
    )
    scale = SHARPNESS * LOG2E / left.shape[1]
    kern = jnp.exp2(gram * scale - SHARPNESS * LOG2E)
    return jnp.where(iota(kern.shape, 1) < count, kern, 0.0)


def folded(kern):
    return functools.reduce(
        jnp.add, [kern[:, c : c + LANES] for c in range(0, kern.shape[1], LANES)]
    )


def terms(left, right, count):
    kern = kernel_tile(left, right, count)
    sums = jnp.dot(kern.astype(jnp.bfloat16), right, preferred_element_type=jnp.float32)
    return folded(kern), sums


def add_terms(x_ref, starts, rights, dens_ref, acc_ref):
    kerns = [
        [kernel_tile(x_ref[pl.ds(start, BLOCK), :], right, count) for right, count in rights]
        for start in starts
    ]
    for start, row in zip(starts, kerns):
        place = pl.ds(start, BLOCK)
        dens_ref[place, :] += functools.reduce(jnp.add, [folded(kern) for kern in row])
        sums = [
            jnp.dot(kern.astype(jnp.bfloat16), right, preferred_element_type=jnp.float32)
            for kern, (right, _) in zip(row, rights)
        ]
        acc_ref[place, :] += functools.reduce(jnp.add, sums)


def add_linked(s, start, other, x_ref, rights, dens_ref, acc_ref):
    @pl.when(s[E0] == 1)
    def _():
        add_terms(x_ref, (start, other), rights, dens_ref, acc_ref)

    @pl.when(s[E0] == 0)
    def _():
        add_terms(x_ref, (start,), rights, dens_ref, acc_ref)


def sibling_links(s, sib_ref):
    tile = sib_ref[pl.ds(2 * BLOCK, TILE), 0:LANES].astype(jnp.float32)
    lane = iota(tile.shape, 1)
    inner = jnp.max(jnp.where(lane == 0, tile, 0.0)) > 0.5
    outer = jnp.max(jnp.where(lane == 1, tile, 0.0)) > 0.5
    return inner, outer


def joined(s, outer):
    return jnp.where(s[PAR] == 1, outer.astype(jnp.int32), s[E1]) == 1


def first_kernel(idx_ref, valid_hbm, embed_ref, first_ref, rows_ref, valid_ref, sems):
    near = idx_ref[0] % 2
    rows = pltpu.make_async_copy(embed_ref.at[pl.ds(at(near), HALF), :], rows_ref, sems.at[0])
    flags = pltpu.make_async_copy(valid_hbm, valid_ref, sems.at[1])
    rows.start()
    flags.start()
    flags.wait()
    place = iota(valid_ref.shape, 0) // (valid_ref.shape[0] // 2)
    real = jnp.sum(jnp.where(place == near, valid_ref[...], 0).astype(jnp.float32))
    rows.wait()
    first_ref[...] = marked(normalized(rows_ref[...]), real.astype(jnp.int32))


def normalize_kernel(
    idx_ref, pairs_hbm, count_ref, valid_hbm, embed_ref, s, x_ref, second_ref,
    rows_ref, valid_ref, pairs_ref, sems
):
    small = [(pairs_hbm, pairs_ref), (valid_hbm, valid_ref)]
    small = [pltpu.make_async_copy(a, b, sems.at[4 + p]) for p, (a, b) in enumerate(small)]
    copies = [
        pltpu.make_async_copy(
            embed_ref.at[pl.ds(p * HALF, HALF), :],
            rows_ref.at[pl.ds(p * HALF, HALF), :],
            sems.at[p],
        )
        for p in range(4)
    ]
    for copy in small + copies:
        copy.start()
    for copy in small:
        copy.wait()
    idx = idx_ref[0]
    counts = [jnp.int32(0), jnp.int32(0)]
    for slot in range(pairs_ref.shape[1]):
        live = slot < count_ref[0]
        for b in range(2):
            hit = jnp.logical_and(live, pairs_ref[0, slot] == idx * 2 + b)
            counts[b] = counts[b] + hit.astype(jnp.int32)
    per = valid_ref.shape[0] // 2
    reals = [
        jnp.sum(valid_ref[b * per : (b + 1) * per, :].astype(jnp.float32)).astype(jnp.int32)
        for b in range(2)
    ]
    links = [(c >= 2).astype(jnp.int32) for c in counts]
    s[IDX] = idx
    s[PAR] = idx % 2
    for b in range(2):
        s[V0 + b] = reals[b]
        s[E0 + b] = links[b]
        s[C0 + b] = counts[b]
    lane = iota((TILE, x_ref.shape[1]), 1)
    flags = jnp.where(
        lane == 0,
        links[0].astype(jnp.float32),
        jnp.where(lane == 1, links[1].astype(jnp.float32), 0.0),
    )
    x_ref[2 * BLOCK :, :] = flags.astype(jnp.bfloat16)
    for p, copy in enumerate(copies):
        copy.wait()
        rows = slice(p * HALF, (p + 1) * HALF)
        count = reals[p // 2] - (p % 2) * HALF
        x_ref[rows, :] = marked(normalized(rows_ref[rows, :]), count)
    apart = jnp.logical_and(idx % 2 == 1, links[1] == 0)
    rows = x_ref[pl.ds(at(idx % 2) + HALF, HALF), :].astype(jnp.float32)
    mark = jnp.where(iota(rows.shape, 1) == 0, 2.0 * MARK, 0.0)
    second_ref[...] = jnp.where(apart, mark, rows).astype(jnp.bfloat16)


def own_block(s, b, x_ref, dens_ref, acc_ref):
    rows = x_ref[b * BLOCK : (b + 1) * BLOCK, :]
    dens, sums = terms(rows, rows, s[V0 + b])
    dens_ref[b * BLOCK : (b + 1) * BLOCK, :] = dens
    acc_ref[b * BLOCK : (b + 1) * BLOCK, :] = sums


def own_kernel(s, x_ref, dens_ref, acc_ref):
    own_block(s, 0, x_ref, dens_ref, acc_ref)


def cross_kernel(s, x_ref, dens_in, acc_in, third_ref, fourth_ref, dens_ref, acc_ref):
    own_block(s, 1, x_ref, dens_ref, acc_ref)
    far = at(1 - s[PAR])
    keep = jnp.logical_and(s[E0] == 1, jnp.logical_or(s[PAR] == 0, s[E1] == 1))
    for half, ref in enumerate((third_ref, fourth_ref)):
        rows = x_ref[pl.ds(far + half * HALF, HALF), :].astype(jnp.float32)
        ref[0:HALF, :] = marked(rows, jnp.where(keep, BLOCK, 0))

    @pl.when(s[E0] == 1)
    def _():
        for b in range(2):
            other = x_ref[(1 - b) * BLOCK : (2 - b) * BLOCK, :]
            add_terms(x_ref, (b * BLOCK,), [(other, s[V0 + 1 - b])], dens_ref, acc_ref)


def add_sibling(s, start, use, x_ref, sib_ref, dens_ref, acc_ref):
    @pl.when(use)
    def _():
        count = real_rows(sib_ref, start, BLOCK)
        rights = [(sib_ref[pl.ds(start, BLOCK), :], count)]
        add_linked(s, at(1 - s[PAR]), at(s[PAR]), x_ref, rights, dens_ref, acc_ref)


def not_apart(qb_ref):
    head = qb_ref[0:TILE, 0:LANES].astype(jnp.float32)
    first = jnp.logical_and(iota(head.shape, 0) == 0, iota(head.shape, 1) == 0)
    return jnp.sum(jnp.where(first, head, 0.0)) < 1.5 * MARK


def across(s, qb_ref):
    below = jnp.logical_and(s[IDX] > 0, not_apart(qb_ref))
    return jnp.where(s[PAR] == 1, s[E1], below.astype(jnp.int32)) == 1


def middle_kernel(s, x_ref, sib_ref, qa_ref, dens_in, acc_in, dens_ref, acc_ref):
    inner, outer = sibling_links(s, sib_ref)
    near, far = at(s[PAR]), at(1 - s[PAR])
    meet = joined(s, outer)
    add_sibling(s, near, meet, x_ref, sib_ref, dens_ref, acc_ref)
    add_sibling(s, far, jnp.logical_and(meet, inner), x_ref, sib_ref, dens_ref, acc_ref)

    @pl.when(jnp.logical_and(s[PAR] == 1, s[E1] == 1))
    def _():
        rights = [(qa_ref[...], real_rows(qa_ref, 0, HALF))]
        add_linked(s, near, far, x_ref, rights, dens_ref, acc_ref)


def sums_go(s):
    return jnp.where(s[PAR] == 1, s[C1] == 2, s[C0] == 3)


def partial_sums(s, q_ref, x_ref, sib_ref, out_ref, dens_ref):
    _, outer = sibling_links(s, sib_ref)
    near, far = at(s[PAR]), at(1 - s[PAR])
    left = q_ref[...]
    count = jnp.where(s[PAR] == 1, s[V0], s[V1]) * s[E0]
    use = jnp.logical_and(s[E0] == 1, joined(s, outer))
    beside = jnp.where(use, real_rows(sib_ref, near, BLOCK), 0)
    rights = [(x_ref[pl.ds(far, BLOCK), :], count), (sib_ref[pl.ds(near, BLOCK), :], beside)]
    kerns = [kernel_tile(left, right, count) for right, count in rights]
    sums = [
        jnp.dot(kern.astype(jnp.bfloat16), right, preferred_element_type=jnp.float32)
        for kern, (right, _) in zip(kerns, rights)
    ]
    dens_ref[...] = folded(kerns[0]) + folded(kerns[1])
    out_ref[0:HALF, :] = (sums[0] + sums[1]).astype(jnp.bfloat16)


def along_lanes(dens):
    return jnp.sum(dens.T, axis=0, keepdims=True)


def third_kernel(s, q_ref, x_ref, sib_ref, out_in, out_ref, dens_ref):
    @pl.when(sums_go(s))
    def _():
        partial_sums(s, q_ref, x_ref, sib_ref, out_ref, dens_ref)


def fourth_kernel(s, q_ref, x_ref, sib_ref, dens_a_ref, out_in, out_ref, dens_ref):
    @pl.when(sums_go(s))
    def _():
        partial_sums(s, q_ref, x_ref, sib_ref, out_ref, dens_ref)
        width = out_ref.shape[1]
        both = [along_lanes(dens_a_ref[...]), along_lanes(dens_ref[...])]
        row = jnp.concatenate(both + [jnp.zeros((1, width - BLOCK), jnp.float32)], axis=1)
        place = iota((TILE, width), 0)
        tile = jnp.zeros((TILE, width), jnp.float32)
        for piece in range(3):
            rounded = row.astype(jnp.bfloat16).astype(jnp.float32)
            tile = jnp.where(place == piece, rounded, tile)
            row = row - rounded
        out_ref[HALF:, :] = tile.astype(jnp.bfloat16)


def outer_kernel(s, x_ref, qa_ref, qb_ref, dens_in, acc_in, came, dens_ref, acc_ref):
    near, far = at(s[PAR]), at(1 - s[PAR])
    linked = across(s, qb_ref)
    upper, lone = s[PAR] == 1, s[E0] == 0
    sums = jnp.where(upper, s[C1] == 4, jnp.logical_and(linked, lone))
    rows = jnp.where(upper, s[C1] == 3, jnp.logical_and(linked, jnp.logical_not(lone)))
    for place in range(8):
        came[place] = s[place]
    came[SUMS] = sums.astype(jnp.int32)
    came[ROWS] = rows.astype(jnp.int32)
    rights = [(ref[...], real_rows(ref, 0, HALF)) for ref in (qa_ref, qb_ref)]

    @pl.when(jnp.logical_and(linked, s[PAR] == 0))
    def _():
        add_linked(s, near, far, x_ref, rights, dens_ref, acc_ref)

    @pl.when(jnp.logical_and(linked, jnp.logical_and(s[PAR] == 1, rights[1][1] > 0)))
    def _():
        add_linked(s, near, far, x_ref, rights[1:], dens_ref, acc_ref)


def forward_kernel(s, x_ref, sib_ref, fa_ref, fb_ref, dens_in, acc_in, dens_ref, acc_ref):
    far = at(1 - s[PAR])
    inner, outer = sibling_links(s, sib_ref)
    below = jnp.logical_and(s[IDX] > 1, not_apart(fb_ref))
    beyond = jnp.where(s[PAR] == 1, below.astype(jnp.int32), outer.astype(jnp.int32)) == 1

    @pl.when(jnp.logical_and(jnp.logical_and(joined(s, outer), inner), beyond))
    def _():
        rights = [(ref[...], real_rows(ref, 0, HALF)) for ref in (fa_ref, fb_ref)]
        add_terms(x_ref, (far,), rights, dens_ref, acc_ref)


def logs_of(density, real):
    use = iota(density.shape, 1) < real
    return jnp.where(use, jnp.log(jnp.where(use, density, 1.0)), 0.0)


def put_logs(log_ref, block, logs):
    per = BLOCK // LANES
    for part in range(per):
        log_ref[pl.ds(block * per + part, 1), :] = logs[:, part * LANES : (part + 1) * LANES]


def finished(sums, start, real):
    return jnp.where(iota(sums.shape, 0) + start < real, sums, 0.0).astype(jnp.bfloat16)


def far_kernel(
    s, x_ref, q_ref, dens_in, acc_in, lanes_ref, log_out, out_ref, dens_ref, acc_ref,
    rows_ref, log_ref, sems
):
    near, far = at(s[PAR]), at(1 - s[PAR])

    @pl.when(s[ROWS] == 1)
    def _():
        count = real_rows(q_ref, 0, HALF)
        add_linked(s, near, far, x_ref, [(q_ref[...], count)], dens_ref, acc_ref)

    @pl.when(s[ROWS] == 0)
    def _():
        @pl.when(s[SUMS] == 1)
        def _():
            acc_ref[pl.ds(near, HALF), :] += q_ref[...].astype(jnp.float32)

        copies = []
        for b in range(2):
            rows = pl.ds(b * BLOCK, BLOCK)
            rows_ref[rows, :] = finished(acc_ref[rows, :], 0, s[V0 + b])
            copy = pltpu.make_async_copy(rows_ref.at[rows, :], out_ref.at[rows, :], sems.at[b])
            copy.start()
            copies.append(copy)
        for b in range(2):
            density = along_lanes(dens_ref[b * BLOCK : (b + 1) * BLOCK, :])
            lanes_ref[b : b + 1, :] = density
            put_logs(log_ref, b, logs_of(density, s[V0 + b]))
        copy = pltpu.make_async_copy(log_ref, log_out, sems.at[2])
        copy.start()
        for copy in copies + [copy]:
            copy.wait()


def last_kernel(
    s, x_ref, q_ref, lanes_ref, dens_ref, acc_ref, log_in, out_in, log_out, out_ref,
    rows_ref, log_ref, sems
):
    log_copy = pltpu.make_async_copy(log_ref, log_out, sems.at[4])

    @pl.when(s[ROWS] == 1)
    def _():
        count = real_rows(q_ref, 0, HALF)
        right = q_ref[0:HALF, :]
        kerns = []
        for b in range(2):
            left = x_ref[b * BLOCK : (b + 1) * BLOCK, :]
            kerns.append(kernel_tile(left, right, jnp.where(s[PAR] == b, count, count * s[E0])))
        copies = []
        for b in range(2):
            for half in range(2):
                rows = pl.ds(b * BLOCK + half * HALF, HALF)
                kern = kerns[b][half * HALF : (half + 1) * HALF].astype(jnp.bfloat16)
                sums = acc_ref[rows, :] + jnp.dot(kern, right, preferred_element_type=jnp.float32)
                rows_ref[rows, :] = finished(sums, half * HALF, s[V0 + b])
                copy = pltpu.make_async_copy(
                    rows_ref.at[rows, :], out_ref.at[rows, :], sems.at[2 * b + half]
                )
                copy.start()
                copies.append(copy)
            if b == 0:
                for c in range(2):
                    density = dens_ref[c * BLOCK : (c + 1) * BLOCK, :] + folded(kerns[c])
                    put_logs(log_ref, c, logs_of(along_lanes(density), s[V0 + c]))
                log_copy.start()
                copies.append(log_copy)
        for copy in copies:
            copy.wait()

    @pl.when(s[SUMS] == 1)
    def _():
        near = at(s[PAR])
        real = jnp.where(s[PAR] == 1, s[V1], s[V0])
        rows = pl.ds(near + HALF, HALF)
        sums = acc_ref[rows, :] + q_ref[0:HALF, :].astype(jnp.float32)
        rows_ref[rows, :] = finished(sums, HALF, real)
        copy = pltpu.make_async_copy(rows_ref.at[rows, :], out_ref.at[rows, :], sems.at[0])
        copy.start()
        tile = q_ref[HALF:, :].astype(jnp.float32)
        pieces = jnp.where(iota(tile.shape, 0) < 3, tile, 0.0)
        more = jnp.sum(pieces, axis=0, keepdims=True)[:, 0:BLOCK]
        for b in range(2):
            density = lanes_ref[b : b + 1, :] + jnp.where(s[PAR] == b, more, 0.0)
            put_logs(log_ref, b, logs_of(density, s[V0 + b]))
        log_copy.start()
        copy.wait()
        log_copy.wait()


def call(kernel, us, in_spaces, operands, outs, out_spaces="", aliases=None, scratch=()):
    spaces = {"s": SM, "v": VM, "h": HB}
    out_spaces = out_spaces or "v" * len(outs)
    return pl.pallas_call(
        kernel,
        in_specs=[spaces[c] for c in in_spaces],
        out_specs=[spaces[c] for c in out_spaces],
        out_shape=outs,
        input_output_aliases=aliases or {},
        scratch_shapes=list(scratch),
        compiler_params=pltpu.CompilerParams(vmem_limit_bytes=16 << 20),
        cost_estimate=pl.CostEstimate(flops=int(us * 1.15e9), bytes_accessed=1 << 10, transcendentals=0),
    )(
        *[
            pltpu.with_memory_space_constraint(x, pltpu.HBM) if c == "h" else x
            for c, x in zip(in_spaces, operands)
        ]
    )


def after(value, *others):
    return lax.optimization_barrier((value, *others))[0]


def per_device(embed, valid, pairs, pair_count):
    width = embed.shape[1]
    chips = lax.axis_size("cluster") // 2
    idx = lax.axis_index("cluster").astype(jnp.int32).reshape(1)
    inchip = [(2 * c + k, 2 * c + 1 - k) for c in range(chips) for k in range(2)]
    edges = [(2 * c + 1, 2 * c + 2) for c in range(chips - 1)]
    edges = edges + [(b, a) for a, b in edges]

    def over_edge(block):
        return lax.ppermute(block, "cluster", edges)

    def to_sibling(block):
        return lax.ppermute(block, "cluster", inchip)

    bf16 = lambda rows: jax.ShapeDtypeStruct((rows, width), jnp.bfloat16)
    f32 = lambda rows, cols: jax.ShapeDtypeStruct((rows, cols), jnp.float32)
    state = [f32(2 * BLOCK, LANES), f32(2 * BLOCK, width)]
    dma = lambda count: pltpu.SemaphoreType.DMA((count,))
    vmem = lambda rows: pltpu.VMEM((rows, width), jnp.bfloat16)

    flags = valid.reshape(-1, LANES)
    (first,) = call(
        first_kernel,
        6.0,
        "shh",
        (idx, flags, embed),
        [bf16(HALF)],
        scratch=(vmem(HALF), pltpu.VMEM(flags.shape, jnp.int32), dma(2)),
    )
    qa = over_edge(first)
    table, x, second = call(
        normalize_kernel,
        14.0,
        "shshh",
        (after(idx, first), pairs.T, pair_count, flags, embed),
        [jax.ShapeDtypeStruct((8,), jnp.int32), bf16(2 * BLOCK + TILE), bf16(HALF)],
        "svv",
        scratch=(
            vmem(2 * BLOCK),
            pltpu.VMEM(flags.shape, jnp.int32),
            pltpu.SMEM(pairs.shape[::-1], jnp.int32),
            dma(6),
        ),
    )
    sib = to_sibling(x)
    dens, acc = call(own_kernel, 30.0, "sv", (table, x), state)
    dens, acc, second = lax.optimization_barrier((dens, acc, second))
    qb = over_edge(second)
    third, fourth, dens, acc = call(
        cross_kernel,
        13.0,
        "svvv",
        (table, x, dens, acc),
        [bf16(HALF), bf16(HALF + TILE)] + state,
        aliases={2: 2, 3: 3},
    )
    third, dens_a = call(
        third_kernel,
        10.0,
        "svvvv",
        (table, qa, x, sib, third),
        [bf16(HALF), f32(HALF, LANES)],
        aliases={4: 0},
    )
    qc = over_edge(third)
    dens, acc, _ = lax.optimization_barrier((dens, acc, third))
    dens, acc = call(
        middle_kernel, 15.0, "svvvvv", (table, x, sib, qa, dens, acc), state, aliases={4: 0, 5: 1}
    )
    (fourth,) = call(
        fourth_kernel,
        10.0,
        "svvvvv",
        (table, qb, after(x, acc), sib, dens_a, fourth),
        [bf16(HALF + TILE)],
        aliases={5: 0},
        scratch=(pltpu.VMEM((HALF, LANES), jnp.float32),),
    )
    dens, acc, fourth = lax.optimization_barrier((dens, acc, fourth))
    qd = over_edge(fourth)
    fa = to_sibling(after(qa, fourth))
    fb = to_sibling(after(qb, fourth))
    came, dens, acc = call(
        outer_kernel,
        15.0,
        "svvvvv",
        (table, x, qa, qb, dens, acc),
        [pltpu.SMEM((10,), jnp.int32)] + state,
        "svv",
        aliases={4: 1, 5: 2},
    )
    dens, acc = call(
        forward_kernel,
        15.0,
        "svvvvvv",
        (table, x, sib, fa, fb, dens, acc),
        state,
        aliases={5: 0, 6: 1},
    )
    log_shape = f32(2 * BLOCK // LANES, LANES)
    lanes, logs, sums, dens, acc = call(
        far_kernel,
        5.0,
        "svvvv",
        (came, x, qc, dens, acc),
        [f32(8, BLOCK), log_shape, bf16(2 * BLOCK)] + state,
        "vhhvv",
        aliases={3: 3, 4: 4},
        scratch=(vmem(2 * BLOCK), pltpu.VMEM(log_shape.shape, jnp.float32), dma(3)),
    )
    logs, sums = call(
        last_kernel,
        5.0,
        "svvvvvhh",
        (came, x, qd, lanes, dens, acc, logs, sums),
        [log_shape, bf16(2 * BLOCK)],
        "hh",
        aliases={6: 0, 7: 1},
        scratch=(vmem(2 * BLOCK), pltpu.VMEM(log_shape.shape, jnp.float32), dma(5)),
    )
    return logs.reshape(-1), sums


def solution(mesh):
    both = ("groups", "cluster")
    return jax.shard_map(
        per_device,
        mesh=mesh,
        in_specs=(P(both, None), P(both), P(both, None), P(both)),
        out_specs=(P(both), P(both, None)),
        check_vma=False,
    )
```

```python
import functools

import jax
import jax.numpy as jnp
from jax import lax
from jax.experimental import pallas as pl
from jax.experimental.pallas import tpu as pltpu
from jax.sharding import PartitionSpec as P

BLOCK = 512
HALF = BLOCK // 2
TILE = 16
LANES = 128
MARK = 100.0
SHARPNESS = 8.0
LOG2E = 1.4426950408889634

IDX, PAR, V0, V1, E0, E1, C0, C1, SUMS, ROWS = range(10)

VM = pl.BlockSpec(memory_space=pltpu.VMEM)
SM = pl.BlockSpec(memory_space=pltpu.SMEM)
HB = pl.BlockSpec(memory_space=pltpu.HBM)


def iota(shape, dim):
    return lax.broadcasted_iota(jnp.int32, shape, dim)


def normalized(rows):
    wide = rows.astype(jnp.float32)
    scale = lax.rsqrt(jnp.mean(wide * wide, axis=-1, keepdims=True) + 1e-06)
    return wide * scale


def marked(rows, count):
    mark = jnp.where(iota(rows.shape, 1) == 0, MARK, 0.0)
    return jnp.where(iota(rows.shape, 0) < count, rows, mark).astype(jnp.bfloat16)


def real_rows(ref, start, rows):
    head = ref[pl.ds(start, rows), 0:LANES].astype(jnp.float32)
    real = jnp.logical_and(iota(head.shape, 1) == 0, head < 0.5 * MARK)
    return jnp.sum(jnp.where(real, 1.0, 0.0)).astype(jnp.int32)


def at(block):
    return pl.multiple_of(block * BLOCK, BLOCK)


def kernel_tile(left, right, count):
    gram = lax.dot_general(
        left, right, (((1,), (1,)), ((), ())), preferred_element_type=jnp.float32
    )
    scale = SHARPNESS * LOG2E / left.shape[1]
    kern = jnp.exp2(gram * scale - SHARPNESS * LOG2E)
    return jnp.where(iota(kern.shape, 1) < count, kern, 0.0)


def folded(kern):
    return functools.reduce(
        jnp.add, [kern[:, c : c + LANES] for c in range(0, kern.shape[1], LANES)]
    )


def terms(left, right, count):
    kern = kernel_tile(left, right, count)
    sums = jnp.dot(kern.astype(jnp.bfloat16), right, preferred_element_type=jnp.float32)
    return folded(kern), sums


def add_terms(x_ref, starts, rights, dens_ref, acc_ref):
    kerns = [
        [kernel_tile(x_ref[pl.ds(start, BLOCK), :], right, count) for right, count in rights]
        for start in starts
    ]
    for start, row in zip(starts, kerns):
        place = pl.ds(start, BLOCK)
        dens_ref[place, :] += functools.reduce(jnp.add, [folded(kern) for kern in row])
        sums = [
            jnp.dot(kern.astype(jnp.bfloat16), right, preferred_element_type=jnp.float32)
            for kern, (right, _) in zip(row, rights)
        ]
        acc_ref[place, :] += functools.reduce(jnp.add, sums)


def add_linked(s, start, other, x_ref, rights, dens_ref, acc_ref):
    @pl.when(s[E0] == 1)
    def _():
        add_terms(x_ref, (start, other), rights, dens_ref, acc_ref)

    @pl.when(s[E0] == 0)
    def _():
        add_terms(x_ref, (start,), rights, dens_ref, acc_ref)


def sibling_links(s, sib_ref):
    tile = sib_ref[pl.ds(2 * BLOCK, TILE), 0:LANES].astype(jnp.float32)
    lane = iota(tile.shape, 1)
    inner = jnp.max(jnp.where(lane == 0, tile, 0.0)) > 0.5
    outer = jnp.max(jnp.where(lane == 1, tile, 0.0)) > 0.5
    return inner, outer


def joined(s, outer):
    return jnp.where(s[PAR] == 1, outer.astype(jnp.int32), s[E1]) == 1


def first_kernel(idx_ref, valid_hbm, embed_ref, first_ref, rows_ref, valid_ref, sems):
    near = idx_ref[0] % 2
    rows = pltpu.make_async_copy(embed_ref.at[pl.ds(at(near), HALF), :], rows_ref, sems.at[0])
    flags = pltpu.make_async_copy(valid_hbm, valid_ref, sems.at[1])
    rows.start()
    flags.start()
    flags.wait()
    place = iota(valid_ref.shape, 0) // (valid_ref.shape[0] // 2)
    real = jnp.sum(jnp.where(place == near, valid_ref[...], 0).astype(jnp.float32))
    rows.wait()
    first_ref[...] = marked(normalized(rows_ref[...]), real.astype(jnp.int32))


def normalize_kernel(
    idx_ref, pairs_hbm, count_ref, valid_hbm, embed_ref, s, x_ref, second_ref,
    rows_ref, valid_ref, pairs_ref, sems
):
    small = [(pairs_hbm, pairs_ref), (valid_hbm, valid_ref)]
    small = [pltpu.make_async_copy(a, b, sems.at[4 + p]) for p, (a, b) in enumerate(small)]
    copies = [
        pltpu.make_async_copy(
            embed_ref.at[pl.ds(p * HALF, HALF), :],
            rows_ref.at[pl.ds(p * HALF, HALF), :],
            sems.at[p],
        )
        for p in range(4)
    ]
    for copy in small + copies:
        copy.start()
    for copy in small:
        copy.wait()
    idx = idx_ref[0]
    counts = [jnp.int32(0), jnp.int32(0)]
    for slot in range(pairs_ref.shape[1]):
        live = slot < count_ref[0]
        for b in range(2):
            hit = jnp.logical_and(live, pairs_ref[0, slot] == idx * 2 + b)
            counts[b] = counts[b] + hit.astype(jnp.int32)
    per = valid_ref.shape[0] // 2
    reals = [
        jnp.sum(valid_ref[b * per : (b + 1) * per, :].astype(jnp.float32)).astype(jnp.int32)
        for b in range(2)
    ]
    links = [(c >= 2).astype(jnp.int32) for c in counts]
    s[IDX] = idx
    s[PAR] = idx % 2
    for b in range(2):
        s[V0 + b] = reals[b]
        s[E0 + b] = links[b]
        s[C0 + b] = counts[b]
    lane = iota((TILE, x_ref.shape[1]), 1)
    flags = jnp.where(
        lane == 0,
        links[0].astype(jnp.float32),
        jnp.where(lane == 1, links[1].astype(jnp.float32), 0.0),
    )
    x_ref[2 * BLOCK :, :] = flags.astype(jnp.bfloat16)
    for p, copy in enumerate(copies):
        copy.wait()
        rows = slice(p * HALF, (p + 1) * HALF)
        count = reals[p // 2] - (p % 2) * HALF
        x_ref[rows, :] = marked(normalized(rows_ref[rows, :]), count)
    apart = jnp.logical_and(idx % 2 == 1, links[1] == 0)
    rows = x_ref[pl.ds(at(idx % 2) + HALF, HALF), :].astype(jnp.float32)
    mark = jnp.where(iota(rows.shape, 1) == 0, 2.0 * MARK, 0.0)
    second_ref[...] = jnp.where(apart, mark, rows).astype(jnp.bfloat16)


def own_block(s, b, x_ref, dens_ref, acc_ref):
    rows = x_ref[b * BLOCK : (b + 1) * BLOCK, :]
    dens, sums = terms(rows, rows, s[V0 + b])
    dens_ref[b * BLOCK : (b + 1) * BLOCK, :] = dens
    acc_ref[b * BLOCK : (b + 1) * BLOCK, :] = sums


def own_kernel(s, x_ref, dens_ref, acc_ref):
    own_block(s, 0, x_ref, dens_ref, acc_ref)


def cross_kernel(s, x_ref, dens_in, acc_in, third_ref, fourth_ref, dens_ref, acc_ref):
    own_block(s, 1, x_ref, dens_ref, acc_ref)
    far = at(1 - s[PAR])
    keep = jnp.logical_and(s[E0] == 1, jnp.logical_or(s[PAR] == 0, s[E1] == 1))
    for half, ref in enumerate((third_ref, fourth_ref)):
        rows = x_ref[pl.ds(far + half * HALF, HALF), :].astype(jnp.float32)
        ref[0:HALF, :] = marked(rows, jnp.where(keep, BLOCK, 0))

    @pl.when(s[E0] == 1)
    def _():
        for b in range(2):
            other = x_ref[(1 - b) * BLOCK : (2 - b) * BLOCK, :]
            add_terms(x_ref, (b * BLOCK,), [(other, s[V0 + 1 - b])], dens_ref, acc_ref)


def add_sibling(s, start, use, x_ref, sib_ref, dens_ref, acc_ref):
    @pl.when(use)
    def _():
        count = real_rows(sib_ref, start, BLOCK)
        rights = [(sib_ref[pl.ds(start, BLOCK), :], count)]
        add_linked(s, at(1 - s[PAR]), at(s[PAR]), x_ref, rights, dens_ref, acc_ref)


def not_apart(qb_ref):
    head = qb_ref[0:TILE, 0:LANES].astype(jnp.float32)
    first = jnp.logical_and(iota(head.shape, 0) == 0, iota(head.shape, 1) == 0)
    return jnp.sum(jnp.where(first, head, 0.0)) < 1.5 * MARK


def across(s, qb_ref):
    below = jnp.logical_and(s[IDX] > 0, not_apart(qb_ref))
    return jnp.where(s[PAR] == 1, s[E1], below.astype(jnp.int32)) == 1


def middle_kernel(s, x_ref, sib_ref, qa_ref, dens_in, acc_in, dens_ref, acc_ref):
    inner, outer = sibling_links(s, sib_ref)
    near, far = at(s[PAR]), at(1 - s[PAR])
    meet = joined(s, outer)
    add_sibling(s, near, meet, x_ref, sib_ref, dens_ref, acc_ref)
    add_sibling(s, far, jnp.logical_and(meet, inner), x_ref, sib_ref, dens_ref, acc_ref)

    @pl.when(jnp.logical_and(s[PAR] == 1, s[E1] == 1))
    def _():
        rights = [(qa_ref[...], real_rows(qa_ref, 0, HALF))]
        add_linked(s, near, far, x_ref, rights, dens_ref, acc_ref)


def sums_go(s):
    return jnp.where(s[PAR] == 1, s[C1] == 2, s[C0] == 3)


def partial_sums(s, q_ref, x_ref, sib_ref, out_ref, dens_ref):
    _, outer = sibling_links(s, sib_ref)
    near, far = at(s[PAR]), at(1 - s[PAR])
    left = q_ref[...]
    count = jnp.where(s[PAR] == 1, s[V0], s[V1]) * s[E0]
    use = jnp.logical_and(s[E0] == 1, joined(s, outer))
    beside = jnp.where(use, real_rows(sib_ref, near, BLOCK), 0)
    rights = [(x_ref[pl.ds(far, BLOCK), :], count), (sib_ref[pl.ds(near, BLOCK), :], beside)]
    kerns = [kernel_tile(left, right, count) for right, count in rights]
    sums = [
        jnp.dot(kern.astype(jnp.bfloat16), right, preferred_element_type=jnp.float32)
        for kern, (right, _) in zip(kerns, rights)
    ]
    dens_ref[...] = folded(kerns[0]) + folded(kerns[1])
    out_ref[0:HALF, :] = (sums[0] + sums[1]).astype(jnp.bfloat16)


def along_lanes(dens):
    return jnp.sum(dens.T, axis=0, keepdims=True)


def third_kernel(s, q_ref, x_ref, sib_ref, out_in, out_ref, dens_ref):
    @pl.when(sums_go(s))
    def _():
        partial_sums(s, q_ref, x_ref, sib_ref, out_ref, dens_ref)


def fourth_kernel(s, q_ref, x_ref, sib_ref, dens_a_ref, out_in, out_ref, tile_ref, dens_ref):
    @pl.when(sums_go(s))
    def _():
        partial_sums(s, q_ref, x_ref, sib_ref, out_ref, dens_ref)
        both = [along_lanes(dens_a_ref[...]), along_lanes(dens_ref[...])]
        row = jnp.concatenate(both, axis=1)
        place = iota(tile_ref.shape, 0)
        tile = jnp.zeros(tile_ref.shape, jnp.float32)
        for piece in range(3):
            rounded = row.astype(jnp.bfloat16).astype(jnp.float32)
            tile = jnp.where(place == piece, rounded, tile)
            row = row - rounded
        tile_ref[...] = tile.astype(jnp.bfloat16)


def outer_kernel(s, x_ref, qa_ref, qb_ref, dens_in, acc_in, came, dens_ref, acc_ref):
    near, far = at(s[PAR]), at(1 - s[PAR])
    linked = across(s, qb_ref)
    upper, lone = s[PAR] == 1, s[E0] == 0
    sums = jnp.where(upper, s[C1] == 4, jnp.logical_and(linked, lone))
    rows = jnp.where(upper, s[C1] == 3, jnp.logical_and(linked, jnp.logical_not(lone)))
    for place in range(8):
        came[place] = s[place]
    came[SUMS] = sums.astype(jnp.int32)
    came[ROWS] = rows.astype(jnp.int32)
    rights = [(ref[...], real_rows(ref, 0, HALF)) for ref in (qa_ref, qb_ref)]

    @pl.when(jnp.logical_and(linked, s[PAR] == 0))
    def _():
        add_linked(s, near, far, x_ref, rights, dens_ref, acc_ref)

    @pl.when(jnp.logical_and(linked, jnp.logical_and(s[PAR] == 1, rights[1][1] > 0)))
    def _():
        add_linked(s, near, far, x_ref, rights[1:], dens_ref, acc_ref)


def forward_kernel(s, x_ref, sib_ref, fa_ref, fb_ref, dens_in, acc_in, dens_ref, acc_ref):
    far = at(1 - s[PAR])
    inner, outer = sibling_links(s, sib_ref)
    below = jnp.logical_and(s[IDX] > 1, not_apart(fb_ref))
    beyond = jnp.where(s[PAR] == 1, below.astype(jnp.int32), outer.astype(jnp.int32)) == 1

    @pl.when(jnp.logical_and(jnp.logical_and(joined(s, outer), inner), beyond))
    def _():
        rights = [(ref[...], real_rows(ref, 0, HALF)) for ref in (fa_ref, fb_ref)]
        add_terms(x_ref, (far,), rights, dens_ref, acc_ref)


def logs_of(density, real):
    use = iota(density.shape, 1) < real
    return jnp.where(use, jnp.log(jnp.where(use, density, 1.0)), 0.0)


def put_logs(log_ref, block, logs):
    per = BLOCK // LANES
    for part in range(per):
        log_ref[pl.ds(block * per + part, 1), :] = logs[:, part * LANES : (part + 1) * LANES]


def finished(sums, start, real):
    return jnp.where(iota(sums.shape, 0) + start < real, sums, 0.0).astype(jnp.bfloat16)


def far_kernel(
    s, x_ref, q_ref, dens_in, acc_in, lanes_ref, log_out, out_ref, dens_ref, acc_ref,
    rows_ref, log_ref, sems
):
    near, far = at(s[PAR]), at(1 - s[PAR])

    @pl.when(s[ROWS] == 1)
    def _():
        count = real_rows(q_ref, 0, HALF)
        add_linked(s, near, far, x_ref, [(q_ref[...], count)], dens_ref, acc_ref)

    @pl.when(s[ROWS] == 0)
    def _():
        @pl.when(s[SUMS] == 1)
        def _():
            acc_ref[pl.ds(near, HALF), :] += q_ref[...].astype(jnp.float32)

        copies = []
        for b in range(2):
            rows = pl.ds(b * BLOCK, BLOCK)
            rows_ref[rows, :] = finished(acc_ref[rows, :], 0, s[V0 + b])
            copy = pltpu.make_async_copy(rows_ref.at[rows, :], out_ref.at[rows, :], sems.at[b])
            copy.start()
            copies.append(copy)
        for b in range(2):
            density = along_lanes(dens_ref[b * BLOCK : (b + 1) * BLOCK, :])
            lanes_ref[b : b + 1, :] = density
            put_logs(log_ref, b, logs_of(density, s[V0 + b]))
        copy = pltpu.make_async_copy(log_ref, log_out, sems.at[2])
        copy.start()
        for copy in copies + [copy]:
            copy.wait()


def last_kernel(
    s, x_ref, q_ref, tile_ref, lanes_ref, dens_ref, acc_ref, log_in, out_in, log_out, out_ref,
    rows_ref, log_ref, sems
):
    log_copy = pltpu.make_async_copy(log_ref, log_out, sems.at[4])

    @pl.when(s[ROWS] == 1)
    def _():
        count = real_rows(q_ref, 0, HALF)
        right = q_ref[0:HALF, :]
        kerns = []
        for b in range(2):
            left = x_ref[b * BLOCK : (b + 1) * BLOCK, :]
            kerns.append(kernel_tile(left, right, jnp.where(s[PAR] == b, count, count * s[E0])))
        copies = []
        for b in range(2):
            for half in range(2):
                rows = pl.ds(b * BLOCK + half * HALF, HALF)
                kern = kerns[b][half * HALF : (half + 1) * HALF].astype(jnp.bfloat16)
                sums = acc_ref[rows, :] + jnp.dot(kern, right, preferred_element_type=jnp.float32)
                rows_ref[rows, :] = finished(sums, half * HALF, s[V0 + b])
                copy = pltpu.make_async_copy(
                    rows_ref.at[rows, :], out_ref.at[rows, :], sems.at[2 * b + half]
                )
                copy.start()
                copies.append(copy)
            if b == 0:
                for c in range(2):
                    density = dens_ref[c * BLOCK : (c + 1) * BLOCK, :] + folded(kerns[c])
                    put_logs(log_ref, c, logs_of(along_lanes(density), s[V0 + c]))
                log_copy.start()
                copies.append(log_copy)
        for copy in copies:
            copy.wait()

    @pl.when(s[SUMS] == 1)
    def _():
        near = at(s[PAR])
        real = jnp.where(s[PAR] == 1, s[V1], s[V0])
        rows = pl.ds(near + HALF, HALF)
        sums = acc_ref[rows, :] + q_ref[0:HALF, :].astype(jnp.float32)
        rows_ref[rows, :] = finished(sums, HALF, real)
        copy = pltpu.make_async_copy(rows_ref.at[rows, :], out_ref.at[rows, :], sems.at[0])
        copy.start()
        pieces = tile_ref[...].astype(jnp.float32)
        pieces = jnp.where(iota(pieces.shape, 0) < 3, pieces, 0.0)
        more = jnp.sum(pieces, axis=0, keepdims=True)
        for b in range(2):
            density = lanes_ref[b : b + 1, :] + jnp.where(s[PAR] == b, more, 0.0)
            put_logs(log_ref, b, logs_of(density, s[V0 + b]))
        log_copy.start()
        copy.wait()
        log_copy.wait()


def call(kernel, us, in_spaces, operands, outs, out_spaces="", aliases=None, scratch=()):
    spaces = {"s": SM, "v": VM, "h": HB}
    out_spaces = out_spaces or "v" * len(outs)
    return pl.pallas_call(
        kernel,
        in_specs=[spaces[c] for c in in_spaces],
        out_specs=[spaces[c] for c in out_spaces],
        out_shape=outs,
        input_output_aliases=aliases or {},
        scratch_shapes=list(scratch),
        compiler_params=pltpu.CompilerParams(vmem_limit_bytes=16 << 20),
        cost_estimate=pl.CostEstimate(flops=int(us * 1.15e9), bytes_accessed=1 << 10, transcendentals=0),
    )(
        *[
            pltpu.with_memory_space_constraint(x, pltpu.HBM) if c == "h" else x
            for c, x in zip(in_spaces, operands)
        ]
    )


def after(value, *others):
    return lax.optimization_barrier((value, *others))[0]


def per_device(embed, valid, pairs, pair_count):
    width = embed.shape[1]
    chips = lax.axis_size("cluster") // 2
    idx = lax.axis_index("cluster").astype(jnp.int32).reshape(1)
    inchip = [(2 * c + k, 2 * c + 1 - k) for c in range(chips) for k in range(2)]
    edges = [(2 * c + 1, 2 * c + 2) for c in range(chips - 1)]
    edges = edges + [(b, a) for a, b in edges]

    def over_edge(block):
        return lax.ppermute(block, "cluster", edges)

    def to_sibling(block):
        return lax.ppermute(block, "cluster", inchip)

    bf16 = lambda rows: jax.ShapeDtypeStruct((rows, width), jnp.bfloat16)
    f32 = lambda rows, cols: jax.ShapeDtypeStruct((rows, cols), jnp.float32)
    state = [f32(2 * BLOCK, LANES), f32(2 * BLOCK, width)]
    dma = lambda count: pltpu.SemaphoreType.DMA((count,))
    vmem = lambda rows: pltpu.VMEM((rows, width), jnp.bfloat16)

    flags = valid.reshape(-1, LANES)
    (first,) = call(
        first_kernel,
        6.0,
        "shh",
        (idx, flags, embed),
        [bf16(HALF)],
        scratch=(vmem(HALF), pltpu.VMEM(flags.shape, jnp.int32), dma(2)),
    )
    qa = over_edge(first)
    table, x, second = call(
        normalize_kernel,
        14.0,
        "shshh",
        (after(idx, first), pairs.T, pair_count, flags, embed),
        [jax.ShapeDtypeStruct((8,), jnp.int32), bf16(2 * BLOCK + TILE), bf16(HALF)],
        "svv",
        scratch=(
            vmem(2 * BLOCK),
            pltpu.VMEM(flags.shape, jnp.int32),
            pltpu.SMEM(pairs.shape[::-1], jnp.int32),
            dma(6),
        ),
    )
    sib = to_sibling(x)
    dens, acc = call(own_kernel, 30.0, "sv", (table, x), state)
    dens, acc, second = lax.optimization_barrier((dens, acc, second))
    qb = over_edge(second)
    third, fourth, dens, acc = call(
        cross_kernel,
        13.0,
        "svvv",
        (table, x, dens, acc),
        [bf16(HALF), bf16(HALF)] + state,
        aliases={2: 2, 3: 3},
    )
    third, dens_a = call(
        third_kernel,
        10.0,
        "svvvv",
        (table, qa, x, sib, third),
        [bf16(HALF), f32(HALF, LANES)],
        aliases={4: 0},
    )
    qc = over_edge(third)
    dens, acc, _ = lax.optimization_barrier((dens, acc, third))
    dens, acc = call(
        middle_kernel, 15.0, "svvvvv", (table, x, sib, qa, dens, acc), state, aliases={4: 0, 5: 1}
    )
    fourth, tile = call(
        fourth_kernel,
        10.0,
        "svvvvv",
        (table, qb, after(x, acc), sib, dens_a, fourth),
        [bf16(HALF), jax.ShapeDtypeStruct((TILE, BLOCK), jnp.bfloat16)],
        aliases={5: 0},
        scratch=(pltpu.VMEM((HALF, LANES), jnp.float32),),
    )
    dens, acc, fourth = lax.optimization_barrier((dens, acc, fourth))
    qd = over_edge(fourth)
    qe = over_edge(after(tile, fourth))
    fa = to_sibling(after(qa, fourth))
    fb = to_sibling(after(qb, fourth))
    came, dens, acc = call(
        outer_kernel,
        15.0,
        "svvvvv",
        (table, x, qa, qb, dens, acc),
        [pltpu.SMEM((10,), jnp.int32)] + state,
        "svv",
        aliases={4: 1, 5: 2},
    )
    dens, acc = call(
        forward_kernel,
        15.0,
        "svvvvvv",
        (table, x, sib, fa, fb, dens, acc),
        state,
        aliases={5: 0, 6: 1},
    )
    log_shape = f32(2 * BLOCK // LANES, LANES)
    lanes, logs, sums, dens, acc = call(
        far_kernel,
        5.0,
        "svvvv",
        (came, x, qc, dens, acc),
        [f32(8, BLOCK), log_shape, bf16(2 * BLOCK)] + state,
        "vhhvv",
        aliases={3: 3, 4: 4},
        scratch=(vmem(2 * BLOCK), pltpu.VMEM(log_shape.shape, jnp.float32), dma(3)),
    )
    logs, sums = call(
        last_kernel,
        5.0,
        "svvvvvvhh",
        (came, x, qd, qe, lanes, dens, acc, logs, sums),
        [log_shape, bf16(2 * BLOCK)],
        "hh",
        aliases={7: 0, 8: 1},
        scratch=(vmem(2 * BLOCK), pltpu.VMEM(log_shape.shape, jnp.float32), dma(5)),
    )
    return logs.reshape(-1), sums


def solution(mesh):
    both = ("groups", "cluster")
    return jax.shard_map(
        per_device,
        mesh=mesh,
        in_specs=(P(both, None), P(both), P(both, None), P(both)),
        out_specs=(P(both), P(both, None)),
        check_vma=False,
    )
```

```python
import functools

import jax
import jax.numpy as jnp
from jax import lax
from jax.experimental import pallas as pl
from jax.experimental.pallas import tpu as pltpu
from jax.sharding import PartitionSpec as P

BLOCK = 512
HALF = BLOCK // 2
TILE = 16
LANES = 128
MARK = 100.0
SHARPNESS = 8.0
LOG2E = 1.4426950408889634

IDX, PAR, V0, V1, E0, E1, C0, C1, SUMS, ROWS = range(10)

VM = pl.BlockSpec(memory_space=pltpu.VMEM)
SM = pl.BlockSpec(memory_space=pltpu.SMEM)
HB = pl.BlockSpec(memory_space=pltpu.HBM)


def iota(shape, dim):
    return lax.broadcasted_iota(jnp.int32, shape, dim)


def normalized(rows):
    wide = rows.astype(jnp.float32)
    scale = lax.rsqrt(jnp.mean(wide * wide, axis=-1, keepdims=True) + 1e-06)
    return wide * scale


def marked(rows, count):
    mark = jnp.where(iota(rows.shape, 1) == 0, MARK, 0.0)
    return jnp.where(iota(rows.shape, 0) < count, rows, mark).astype(jnp.bfloat16)


def real_rows(ref, start, rows):
    head = ref[pl.ds(start, rows), 0:LANES].astype(jnp.float32)
    real = jnp.logical_and(iota(head.shape, 1) == 0, head < 0.5 * MARK)
    return jnp.sum(jnp.where(real, 1.0, 0.0)).astype(jnp.int32)


def at(block):
    return pl.multiple_of(block * BLOCK, BLOCK)


def kernel_tile(left, right, count):
    gram = lax.dot_general(
        left, right, (((1,), (1,)), ((), ())), preferred_element_type=jnp.float32
    )
    scale = SHARPNESS * LOG2E / left.shape[1]
    kern = jnp.exp2(gram * scale - SHARPNESS * LOG2E)
    return jnp.where(iota(kern.shape, 1) < count, kern, 0.0)


def folded(kern):
    return functools.reduce(
        jnp.add, [kern[:, c : c + LANES] for c in range(0, kern.shape[1], LANES)]
    )


def terms(left, right, count):
    kern = kernel_tile(left, right, count)
    sums = jnp.dot(kern.astype(jnp.bfloat16), right, preferred_element_type=jnp.float32)
    return folded(kern), sums


def add_terms(x_ref, starts, rights, dens_ref, acc_ref):
    kerns = [
        [kernel_tile(x_ref[pl.ds(start, BLOCK), :], right, count) for right, count in rights]
        for start in starts
    ]
    for start, row in zip(starts, kerns):
        place = pl.ds(start, BLOCK)
        dens_ref[place, :] += functools.reduce(jnp.add, [folded(kern) for kern in row])
        sums = [
            jnp.dot(kern.astype(jnp.bfloat16), right, preferred_element_type=jnp.float32)
            for kern, (right, _) in zip(row, rights)
        ]
        acc_ref[place, :] += functools.reduce(jnp.add, sums)


def add_linked(s, start, other, x_ref, rights, dens_ref, acc_ref):
    @pl.when(s[E0] == 1)
    def _():
        add_terms(x_ref, (start, other), rights, dens_ref, acc_ref)

    @pl.when(s[E0] == 0)
    def _():
        add_terms(x_ref, (start,), rights, dens_ref, acc_ref)


def sibling_links(s, sib_ref):
    tile = sib_ref[pl.ds(2 * BLOCK, TILE), 0:LANES].astype(jnp.float32)
    lane = iota(tile.shape, 1)
    inner = jnp.max(jnp.where(lane == 0, tile, 0.0)) > 0.5
    outer = jnp.max(jnp.where(lane == 1, tile, 0.0)) > 0.5
    return inner, outer


def joined(s, outer):
    return jnp.where(s[PAR] == 1, outer.astype(jnp.int32), s[E1]) == 1


def first_kernel(idx_ref, valid_hbm, embed_ref, first_ref, rows_ref, valid_ref, sems):
    near = idx_ref[0] % 2
    rows = pltpu.make_async_copy(embed_ref.at[pl.ds(at(near), HALF), :], rows_ref, sems.at[0])
    flags = pltpu.make_async_copy(valid_hbm, valid_ref, sems.at[1])
    rows.start()
    flags.start()
    flags.wait()
    place = iota(valid_ref.shape, 0) // (valid_ref.shape[0] // 2)
    real = jnp.sum(jnp.where(place == near, valid_ref[...], 0).astype(jnp.float32))
    rows.wait()
    first_ref[...] = marked(normalized(rows_ref[...]), real.astype(jnp.int32))


def normalize_kernel(
    idx_ref, pairs_hbm, count_ref, valid_hbm, embed_ref, s, x_ref, second_ref,
    rows_ref, valid_ref, pairs_ref, sems
):
    small = [(pairs_hbm, pairs_ref), (valid_hbm, valid_ref)]
    small = [pltpu.make_async_copy(a, b, sems.at[4 + p]) for p, (a, b) in enumerate(small)]
    copies = [
        pltpu.make_async_copy(
            embed_ref.at[pl.ds(p * HALF, HALF), :],
            rows_ref.at[pl.ds(p * HALF, HALF), :],
            sems.at[p],
        )
        for p in range(4)
    ]
    for copy in small + copies:
        copy.start()
    for copy in small:
        copy.wait()
    idx = idx_ref[0]
    counts = [jnp.int32(0), jnp.int32(0)]
    for slot in range(pairs_ref.shape[1]):
        live = slot < count_ref[0]
        for b in range(2):
            hit = jnp.logical_and(live, pairs_ref[0, slot] == idx * 2 + b)
            counts[b] = counts[b] + hit.astype(jnp.int32)
    per = valid_ref.shape[0] // 2
    reals = [
        jnp.sum(valid_ref[b * per : (b + 1) * per, :].astype(jnp.float32)).astype(jnp.int32)
        for b in range(2)
    ]
    links = [(c >= 2).astype(jnp.int32) for c in counts]
    s[IDX] = idx
    s[PAR] = idx % 2
    for b in range(2):
        s[V0 + b] = reals[b]
        s[E0 + b] = links[b]
        s[C0 + b] = counts[b]
    lane = iota((TILE, x_ref.shape[1]), 1)
    flags = jnp.where(
        lane == 0,
        links[0].astype(jnp.float32),
        jnp.where(lane == 1, links[1].astype(jnp.float32), 0.0),
    )
    x_ref[2 * BLOCK :, :] = flags.astype(jnp.bfloat16)
    for p, copy in enumerate(copies):
        copy.wait()
        rows = slice(p * HALF, (p + 1) * HALF)
        count = reals[p // 2] - (p % 2) * HALF
        x_ref[rows, :] = marked(normalized(rows_ref[rows, :]), count)
    apart = jnp.logical_and(idx % 2 == 1, links[1] == 0)
    rows = x_ref[pl.ds(at(idx % 2) + HALF, HALF), :].astype(jnp.float32)
    mark = jnp.where(iota(rows.shape, 1) == 0, 2.0 * MARK, 0.0)
    second_ref[...] = jnp.where(apart, mark, rows).astype(jnp.bfloat16)


def own_block(s, b, x_ref, dens_ref, acc_ref):
    rows = x_ref[b * BLOCK : (b + 1) * BLOCK, :]
    dens, sums = terms(rows, rows, s[V0 + b])
    dens_ref[b * BLOCK : (b + 1) * BLOCK, :] = dens
    acc_ref[b * BLOCK : (b + 1) * BLOCK, :] = sums


def own_kernel(s, x_ref, dens_ref, acc_ref):
    own_block(s, 0, x_ref, dens_ref, acc_ref)


def cross_kernel(s, x_ref, dens_in, acc_in, third_ref, fourth_ref, dens_ref, acc_ref):
    own_block(s, 1, x_ref, dens_ref, acc_ref)
    far = at(1 - s[PAR])
    keep = jnp.logical_and(s[E0] == 1, jnp.logical_or(s[PAR] == 0, s[E1] == 1))
    for half, ref in enumerate((third_ref, fourth_ref)):
        rows = x_ref[pl.ds(far + half * HALF, HALF), :].astype(jnp.float32)
        ref[0:HALF, :] = marked(rows, jnp.where(keep, BLOCK, 0))

    @pl.when(s[E0] == 1)
    def _():
        for b in range(2):
            other = x_ref[(1 - b) * BLOCK : (2 - b) * BLOCK, :]
            add_terms(x_ref, (b * BLOCK,), [(other, s[V0 + 1 - b])], dens_ref, acc_ref)


def add_sibling(s, start, use, x_ref, sib_ref, dens_ref, acc_ref):
    @pl.when(use)
    def _():
        count = real_rows(sib_ref, start, BLOCK)
        rights = [(sib_ref[pl.ds(start, BLOCK), :], count)]
        add_linked(s, at(1 - s[PAR]), at(s[PAR]), x_ref, rights, dens_ref, acc_ref)


def not_apart(qb_ref):
    head = qb_ref[0:TILE, 0:LANES].astype(jnp.float32)
    first = jnp.logical_and(iota(head.shape, 0) == 0, iota(head.shape, 1) == 0)
    return jnp.sum(jnp.where(first, head, 0.0)) < 1.5 * MARK


def across(s, qb_ref):
    below = jnp.logical_and(s[IDX] > 0, not_apart(qb_ref))
    return jnp.where(s[PAR] == 1, s[E1], below.astype(jnp.int32)) == 1


def middle_kernel(s, x_ref, sib_ref, qa_ref, dens_in, acc_in, dens_ref, acc_ref):
    inner, outer = sibling_links(s, sib_ref)
    near, far = at(s[PAR]), at(1 - s[PAR])
    meet = joined(s, outer)
    add_sibling(s, near, meet, x_ref, sib_ref, dens_ref, acc_ref)
    add_sibling(s, far, jnp.logical_and(meet, inner), x_ref, sib_ref, dens_ref, acc_ref)

    @pl.when(jnp.logical_and(s[PAR] == 1, s[E1] == 1))
    def _():
        rights = [(qa_ref[...], real_rows(qa_ref, 0, HALF))]
        add_linked(s, near, far, x_ref, rights, dens_ref, acc_ref)


def sums_go(s):
    return jnp.where(s[PAR] == 1, s[C1] == 2, s[C0] == 3)


def partial_sums(s, q_ref, x_ref, sib_ref, out_ref, dens_ref):
    _, outer = sibling_links(s, sib_ref)
    near, far = at(s[PAR]), at(1 - s[PAR])
    left = q_ref[...]
    count = jnp.where(s[PAR] == 1, s[V0], s[V1]) * s[E0]
    use = jnp.logical_and(s[E0] == 1, joined(s, outer))
    beside = jnp.where(use, real_rows(sib_ref, near, BLOCK), 0)
    rights = [(x_ref[pl.ds(far, BLOCK), :], count), (sib_ref[pl.ds(near, BLOCK), :], beside)]
    kerns = [kernel_tile(left, right, count) for right, count in rights]
    sums = [
        jnp.dot(kern.astype(jnp.bfloat16), right, preferred_element_type=jnp.float32)
        for kern, (right, _) in zip(kerns, rights)
    ]
    dens_ref[...] = folded(kerns[0]) + folded(kerns[1])
    out_ref[0:HALF, :] = (sums[0] + sums[1]).astype(jnp.bfloat16)


def along_lanes(dens):
    return jnp.sum(dens.T, axis=0, keepdims=True)


def third_kernel(s, q_ref, x_ref, sib_ref, out_in, out_ref, dens_ref):
    @pl.when(sums_go(s))
    def _():
        partial_sums(s, q_ref, x_ref, sib_ref, out_ref, dens_ref)


def fourth_kernel(s, q_ref, x_ref, sib_ref, dens_a_ref, out_in, out_ref, tile_ref, dens_ref):
    @pl.when(sums_go(s))
    def _():
        partial_sums(s, q_ref, x_ref, sib_ref, out_ref, dens_ref)
        both = [along_lanes(dens_a_ref[...]), along_lanes(dens_ref[...])]
        row = jnp.concatenate(both, axis=1)
        place = iota(tile_ref.shape, 0)
        tile = jnp.zeros(tile_ref.shape, jnp.float32)
        for piece in range(3):
            rounded = row.astype(jnp.bfloat16).astype(jnp.float32)
            tile = jnp.where(place == piece, rounded, tile)
            row = row - rounded
        tile_ref[...] = tile.astype(jnp.bfloat16)


def outer_kernel(s, x_ref, qa_ref, qb_ref, dens_in, acc_in, came, dens_ref, acc_ref):
    near, far = at(s[PAR]), at(1 - s[PAR])
    linked = across(s, qb_ref)
    upper, lone = s[PAR] == 1, s[E0] == 0
    sums = jnp.where(upper, s[C1] == 4, jnp.logical_and(linked, lone))
    rows = jnp.where(upper, s[C1] == 3, jnp.logical_and(linked, jnp.logical_not(lone)))
    for place in range(8):
        came[place] = s[place]
    came[SUMS] = sums.astype(jnp.int32)
    came[ROWS] = rows.astype(jnp.int32)
    rights = [(ref[...], real_rows(ref, 0, HALF)) for ref in (qa_ref, qb_ref)]

    @pl.when(jnp.logical_and(linked, s[PAR] == 0))
    def _():
        add_linked(s, near, far, x_ref, rights, dens_ref, acc_ref)

    @pl.when(jnp.logical_and(linked, jnp.logical_and(s[PAR] == 1, rights[1][1] > 0)))
    def _():
        add_linked(s, near, far, x_ref, rights[1:], dens_ref, acc_ref)


def forward_kernel(s, x_ref, sib_ref, fa_ref, fb_ref, dens_in, acc_in, dens_ref, acc_ref):
    far = at(1 - s[PAR])
    inner, outer = sibling_links(s, sib_ref)
    below = jnp.logical_and(s[IDX] > 1, not_apart(fb_ref))
    beyond = jnp.where(s[PAR] == 1, below.astype(jnp.int32), outer.astype(jnp.int32)) == 1

    @pl.when(jnp.logical_and(jnp.logical_and(joined(s, outer), inner), beyond))
    def _():
        rights = [(ref[...], real_rows(ref, 0, HALF)) for ref in (fa_ref, fb_ref)]
        add_terms(x_ref, (far,), rights, dens_ref, acc_ref)


def logs_of(density, real):
    use = iota(density.shape, 1) < real
    return jnp.where(use, jnp.log(jnp.where(use, density, 1.0)), 0.0)


def put_logs(log_ref, block, logs):
    per = BLOCK // LANES
    for part in range(per):
        log_ref[pl.ds(block * per + part, 1), :] = logs[:, part * LANES : (part + 1) * LANES]


def finished(sums, start, real):
    return jnp.where(iota(sums.shape, 0) + start < real, sums, 0.0).astype(jnp.bfloat16)


def far_kernel(
    s, x_ref, q_ref, dens_in, acc_in, lanes_ref, log_out, out_ref, dens_ref, acc_ref,
    rows_ref, log_ref, sems
):
    near, far = at(s[PAR]), at(1 - s[PAR])

    @pl.when(s[ROWS] == 1)
    def _():
        count = real_rows(q_ref, 0, HALF)
        add_linked(s, near, far, x_ref, [(q_ref[...], count)], dens_ref, acc_ref)

    @pl.when(s[ROWS] == 0)
    def _():
        @pl.when(s[SUMS] == 1)
        def _():
            acc_ref[pl.ds(near, HALF), :] += q_ref[...].astype(jnp.float32)

        copies = []
        for b in range(2):
            rows = pl.ds(b * BLOCK, BLOCK)
            rows_ref[rows, :] = finished(acc_ref[rows, :], 0, s[V0 + b])
            copy = pltpu.make_async_copy(rows_ref.at[rows, :], out_ref.at[rows, :], sems.at[b])
            copy.start()
            copies.append(copy)
        for b in range(2):
            density = along_lanes(dens_ref[b * BLOCK : (b + 1) * BLOCK, :])
            lanes_ref[b : b + 1, :] = density
            put_logs(log_ref, b, logs_of(density, s[V0 + b]))
        copy = pltpu.make_async_copy(log_ref, log_out, sems.at[2])
        copy.start()
        for copy in copies + [copy]:
            copy.wait()


def last_kernel(
    s, x_ref, q_ref, tile_ref, lanes_ref, dens_ref, acc_ref, log_in, out_in, log_out, out_ref,
    rows_ref, log_ref, sems
):
    log_copy = pltpu.make_async_copy(log_ref, log_out, sems.at[4])

    @pl.when(s[ROWS] == 1)
    def _():
        count = real_rows(q_ref, 0, HALF)
        right = q_ref[0:HALF, :]
        counts = [jnp.where(s[PAR] == b, count, count * s[E0]) for b in range(2)]
        copies = []

        def finish(start, rows, kern):
            place = pl.ds(start, rows)
            sums = acc_ref[place, :] + jnp.dot(
                kern.astype(jnp.bfloat16), right, preferred_element_type=jnp.float32
            )
            rows_ref[place, :] = finished(sums, start % BLOCK, s[V0 + start // BLOCK])
            copy = pltpu.make_async_copy(
                rows_ref.at[place, :], out_ref.at[place, :], sems.at[start // HALF]
            )
            copy.start()
            copies.append(copy)

        def log_block(b, density):
            put_logs(log_ref, b, logs_of(along_lanes(density), s[V0 + b]))

        kerns = []
        for t in range(4):
            place = pl.ds(t * HALF, HALF)
            kerns.append(kernel_tile(x_ref[place, :], right, counts[t // 2]))
            if t:
                finish((t - 1) * HALF, HALF, kerns[t - 1])
        for b in range(2):
            density = [
                dens_ref[pl.ds(t * HALF, HALF), :] + folded(kerns[t]) for t in (2 * b, 2 * b + 1)
            ]
            log_block(b, jnp.concatenate(density, axis=0))
        log_copy.start()
        copies.append(log_copy)
        finish(3 * HALF, HALF, kerns[3])
        for copy in copies:
            copy.wait()

    @pl.when(s[SUMS] == 1)
    def _():
        near = at(s[PAR])
        real = jnp.where(s[PAR] == 1, s[V1], s[V0])
        rows = pl.ds(near + HALF, HALF)
        sums = acc_ref[rows, :] + q_ref[0:HALF, :].astype(jnp.float32)
        rows_ref[rows, :] = finished(sums, HALF, real)
        copy = pltpu.make_async_copy(rows_ref.at[rows, :], out_ref.at[rows, :], sems.at[0])
        copy.start()
        pieces = tile_ref[...].astype(jnp.float32)
        pieces = jnp.where(iota(pieces.shape, 0) < 3, pieces, 0.0)
        more = jnp.sum(pieces, axis=0, keepdims=True)
        for b in range(2):
            density = lanes_ref[b : b + 1, :] + jnp.where(s[PAR] == b, more, 0.0)
            put_logs(log_ref, b, logs_of(density, s[V0 + b]))
        log_copy.start()
        copy.wait()
        log_copy.wait()


def call(kernel, us, in_spaces, operands, outs, out_spaces="", aliases=None, scratch=()):
    spaces = {"s": SM, "v": VM, "h": HB}
    out_spaces = out_spaces or "v" * len(outs)
    return pl.pallas_call(
        kernel,
        in_specs=[spaces[c] for c in in_spaces],
        out_specs=[spaces[c] for c in out_spaces],
        out_shape=outs,
        input_output_aliases=aliases or {},
        scratch_shapes=list(scratch),
        compiler_params=pltpu.CompilerParams(vmem_limit_bytes=16 << 20),
        cost_estimate=pl.CostEstimate(flops=int(us * 1.15e9), bytes_accessed=1 << 10, transcendentals=0),
    )(
        *[
            pltpu.with_memory_space_constraint(x, pltpu.HBM) if c == "h" else x
            for c, x in zip(in_spaces, operands)
        ]
    )


def after(value, *others):
    return lax.optimization_barrier((value, *others))[0]


def per_device(embed, valid, pairs, pair_count):
    width = embed.shape[1]
    chips = lax.axis_size("cluster") // 2
    idx = lax.axis_index("cluster").astype(jnp.int32).reshape(1)
    inchip = [(2 * c + k, 2 * c + 1 - k) for c in range(chips) for k in range(2)]
    edges = [(2 * c + 1, 2 * c + 2) for c in range(chips - 1)]
    edges = edges + [(b, a) for a, b in edges]

    def over_edge(block):
        return lax.ppermute(block, "cluster", edges)

    def to_sibling(block):
        return lax.ppermute(block, "cluster", inchip)

    bf16 = lambda rows: jax.ShapeDtypeStruct((rows, width), jnp.bfloat16)
    f32 = lambda rows, cols: jax.ShapeDtypeStruct((rows, cols), jnp.float32)
    state = [f32(2 * BLOCK, LANES), f32(2 * BLOCK, width)]
    dma = lambda count: pltpu.SemaphoreType.DMA((count,))
    vmem = lambda rows: pltpu.VMEM((rows, width), jnp.bfloat16)

    flags = valid.reshape(-1, LANES)
    (first,) = call(
        first_kernel,
        6.0,
        "shh",
        (idx, flags, embed),
        [bf16(HALF)],
        scratch=(vmem(HALF), pltpu.VMEM(flags.shape, jnp.int32), dma(2)),
    )
    qa = over_edge(first)
    table, x, second = call(
        normalize_kernel,
        14.0,
        "shshh",
        (after(idx, first), pairs.T, pair_count, flags, embed),
        [jax.ShapeDtypeStruct((8,), jnp.int32), bf16(2 * BLOCK + TILE), bf16(HALF)],
        "svv",
        scratch=(
            vmem(2 * BLOCK),
            pltpu.VMEM(flags.shape, jnp.int32),
            pltpu.SMEM(pairs.shape[::-1], jnp.int32),
            dma(6),
        ),
    )
    sib = to_sibling(x)
    dens, acc = call(own_kernel, 30.0, "sv", (table, x), state)
    dens, acc, second = lax.optimization_barrier((dens, acc, second))
    qb = over_edge(second)
    third, fourth, dens, acc = call(
        cross_kernel,
        13.0,
        "svvv",
        (table, x, dens, acc),
        [bf16(HALF), bf16(HALF)] + state,
        aliases={2: 2, 3: 3},
    )
    third, dens_a = call(
        third_kernel,
        10.0,
        "svvvv",
        (table, qa, x, sib, third),
        [bf16(HALF), f32(HALF, LANES)],
        aliases={4: 0},
    )
    qc = over_edge(third)
    dens, acc, _ = lax.optimization_barrier((dens, acc, third))
    dens, acc = call(
        middle_kernel, 15.0, "svvvvv", (table, x, sib, qa, dens, acc), state, aliases={4: 0, 5: 1}
    )
    fourth, tile = call(
        fourth_kernel,
        10.0,
        "svvvvv",
        (table, qb, after(x, acc), sib, dens_a, fourth),
        [bf16(HALF), jax.ShapeDtypeStruct((TILE, BLOCK), jnp.bfloat16)],
        aliases={5: 0},
        scratch=(pltpu.VMEM((HALF, LANES), jnp.float32),),
    )
    dens, acc, fourth = lax.optimization_barrier((dens, acc, fourth))
    qd = over_edge(fourth)
    qe = over_edge(after(tile, fourth))
    fa = to_sibling(after(qa, fourth))
    fb = to_sibling(after(qb, fourth))
    came, dens, acc = call(
        outer_kernel,
        15.0,
        "svvvvv",
        (table, x, qa, qb, dens, acc),
        [pltpu.SMEM((10,), jnp.int32)] + state,
        "svv",
        aliases={4: 1, 5: 2},
    )
    dens, acc = call(
        forward_kernel,
        15.0,
        "svvvvvv",
        (table, x, sib, fa, fb, dens, acc),
        state,
        aliases={5: 0, 6: 1},
    )
    log_shape = f32(2 * BLOCK // LANES, LANES)
    lanes, logs, sums, dens, acc = call(
        far_kernel,
        5.0,
        "svvvv",
        (came, x, qc, dens, acc),
        [f32(8, BLOCK), log_shape, bf16(2 * BLOCK)] + state,
        "vhhvv",
        aliases={3: 3, 4: 4},
        scratch=(vmem(2 * BLOCK), pltpu.VMEM(log_shape.shape, jnp.float32), dma(3)),
    )
    logs, sums = call(
        last_kernel,
        5.0,
        "svvvvvvhh",
        (came, x, qd, qe, lanes, dens, acc, logs, sums),
        [log_shape, bf16(2 * BLOCK)],
        "hh",
        aliases={7: 0, 8: 1},
        scratch=(vmem(2 * BLOCK), pltpu.VMEM(log_shape.shape, jnp.float32), dma(5)),
    )
    return logs.reshape(-1), sums


def solution(mesh):
    both = ("groups", "cluster")
    return jax.shard_map(
        per_device,
        mesh=mesh,
        in_specs=(P(both, None), P(both), P(both, None), P(both)),
        out_specs=(P(both), P(both, None)),
        check_vma=False,
    )
```
